32 devices in a mesh: groups: 2 (over x), row: 16 (over z, y, core).
Axes of the slice: x: 2, y: 2, z: 4, core: 2. Of those that a mesh axis runs over, the one named last changes fastest.
Arguments:
- pair: bfloat16 [4, 128, 64, 128], P('groups', 'row'), parts along dimension 0, may hold values from -6 to 6
- cotangent: bfloat16 [4, 128, 64, 128], P('groups', 'row'), parts along dimension 0, may hold values from -6 to 6
- token_mask: int32 [256], P('groups'), parts along dimension 0, may hold values 0 or 1
- coverage: int32 [4, 1, 1], P('groups'), parts along dimension 0, may hold values 0 or 1
- w_proj: bfloat16 [4, 64, 64], replicated, may hold values from -0.75 to 0.75
- w_out: bfloat16 [2, 64, 64], replicated, may hold values from -0.75 to 0.75
- layer_norm_gains: float32 [2, 64], replicated, may hold values from 0.1 to 1.9
- ln_bias: float32 [64], replicated, may hold values from -3 to 3
Outputs:
- pair_grad: bfloat16 [4, 128, 64, 128], P('groups', 'row'), parts along dimension 0
- grad_proj: float32 [8, 64, 64], P('groups'), parts along dimension 0
- grad_out: float32 [4, 64, 64], P('groups'), parts along dimension 0
- norm_gain_gradients: float32 [6, 64], P('groups'), parts along dimension 0
The draws below stay inside these ranges and needn't reach their ends.
There are 2 independent parts, one for each index of `groups`. The reference program is written for one: setup_inputs(seed, part) draws one part's arguments, and reference() takes and returns one part's arrays. A program takes and returns all parts, laid end to end along the dimension named above; an argument that names none is the same for every part. Nothing has to cross between parts.
All inputs are finite; a program needn't handle non-finite values.
Results may differ from the reference program's by a relative error of at most 0.014.
Values may be sent and summed in bfloat16 or wider, within the bound.
No kernel may reach another device: no remote copies, remote signals or barrier semaphores. Data moves between devices by JAX's collectives and lax.ppermute only.
A program may use at most 128 MiB of HBM per device.

```python
import jax
import jax.numpy as jnp
from jax import lax

C = 64
TEMPL = 2
TILE = 128
N = 128


def touch_ends(drawn, stream_key, low, top_value):
    longest = drawn.shape.index(max(drawn.shape))
    spots = []
    for shift in (0, 1):
        where = [jax.random.randint(jax.random.fold_in(stream_key, axis), (), 0, length) for axis, length in enumerate(drawn.shape)]
        where[longest] = (where[longest] + shift) % drawn.shape[longest]
        spots.append(tuple(where))
    return drawn.at[spots[0]].set(low).at[spots[1]].set(top_value)


def level_of(rng, shape, pieces, smallest, high):
    def one(axis_at, parts):
        heights = jax.random.uniform(jax.random.fold_in(jax.random.fold_in(rng, 6), axis_at), (parts,), jnp.float32, smallest / len(pieces), high / len(pieces))
        return jnp.repeat(jnp.exp(heights), shape[axis_at] // parts).reshape((-1,) + (1,) * (len(shape) - axis_at - 1))

    loudness = one(*pieces[0])
    for cut in pieces[1:]:
        loudness = loudness * one(*cut)
    return loudness


def noise(key, shape, width, bound, pieces=(), kind=jnp.bfloat16):
    level = level_of(key, shape, pieces, -0.22, 0.18) if pieces else 1.0
    values = jax.random.normal(key, shape, jnp.float32) * width * level
    return jnp.minimum(jnp.maximum(values, -bound), bound).astype(kind)


def setup_inputs(seed: int = 0, part: int = 0) -> dict:
    keys = jax.random.split(jax.random.key(seed), 9)
    part_keys = jax.random.split(jax.random.fold_in(keys[8], part), 9)
    return {
        "pair": noise(part_keys[0], (TEMPL, N, C, N), 1.0, 6.0, ((1, 16),)),
        "cotangent": noise(part_keys[1], (TEMPL, N, C, N), 1.0, 6.0, ((1, 16),)),
        "token_mask": touch_ends((jax.random.randint(part_keys[2], (N,), 0, 8) < 7).astype(jnp.int32), jax.random.fold_in(part_keys[2], 1), 0, 1),
        "coverage": touch_ends((jax.random.randint(part_keys[3], (TEMPL, N // TILE, N // TILE), 0, 4) < 3).astype(jnp.int32), jax.random.fold_in(part_keys[3], 1), 0, 1),
        "w_proj": noise(keys[4], (4, C, C), C ** -0.5, 0.75),
        "w_out": noise(keys[5], (2, C, C), C ** -0.5, 0.75),
        "layer_norm_gains": jnp.clip(1.0 + 0.18 * jax.random.normal(keys[6], (2, C), jnp.float32), 0.1, 1.9),
        "ln_bias": noise(keys[7], (C,), 0.5, 3.0, (), jnp.float32),
    }


EPS = 1e-05

def apply_layer_norm(values):
    mean = lax.optimization_barrier(jnp.mean(values, axis=1, keepdims=True))
    centred = values - mean
    rstd = lax.rsqrt(lax.optimization_barrier(jnp.mean(centred * centred, axis=1, keepdims=True)) + EPS)
    return (centred * rstd, rstd)

def layer_norm_backward(grad, normed_values, rstd):
    mean_grad = lax.optimization_barrier(jnp.mean(grad, axis=1, keepdims=True))
    mean_proj = lax.optimization_barrier(jnp.mean(grad * normed_values, axis=1, keepdims=True))
    return rstd * (grad - mean_grad - normed_values * mean_proj)

def channel_map(weight, values):
    return jnp.einsum('co,ick->iok', weight.astype(jnp.float32), values.astype(jnp.float32))

def channel_back(weight, grads):
    return jnp.einsum('co,iok->ick', weight.astype(jnp.float32), grads.astype(jnp.float32))

def weight_grad(inputs, grads):
    return jnp.einsum('ick,iok->co', inputs.astype(jnp.float32), grads.astype(jnp.float32))

def tile_cover(token_mask, cover_one):
    maskf = token_mask.astype(jnp.float32)
    count = token_mask.shape[0]
    tiles = cover_one.shape[0]
    row_ids = jnp.arange(count, dtype=jnp.int32)
    onehot = (row_ids[:, None] // TILE == jnp.arange(tiles, dtype=jnp.int32)[None, :]).astype(jnp.float32)
    row_cov = jnp.dot(onehot, cover_one.astype(jnp.float32))
    columns = jnp.repeat(row_cov, TILE, axis=1)
    return columns * maskf[:, None] * maskf[None, :]

def gating_back(grad, gate_pre, value_pre, mask):
    sig = jax.nn.sigmoid(gate_pre)
    d_gate = (grad * value_pre * mask * sig * (1.0 - sig)).astype(jnp.bfloat16)
    d_value = (grad * sig * mask).astype(jnp.bfloat16)
    return [d_gate, d_value]

def reference(pair, cotangent, token_mask, coverage, w_proj, w_out, layer_norm_gains, ln_bias):

    def one_template(items):
        pair_one, cot_one, cover_one = items
        normed_values, rstd = apply_layer_norm(pair_one.astype(jnp.float32))
        zn = (normed_values * layer_norm_gains[0][:, None] + ln_bias[:, None]).astype(jnp.bfloat16)
        mask = tile_cover(token_mask, cover_one)[:, None, :]
        pre = [channel_map(w_proj[p], zn) for p in range(4)]
        left = (jax.nn.sigmoid(pre[0]) * pre[1] * mask).astype(jnp.bfloat16)
        right = (jax.nn.sigmoid(pre[2]) * pre[3] * mask).astype(jnp.bfloat16)
        mixed_product = jnp.einsum('ick,jck->icj', left.astype(jnp.float32), right.astype(jnp.float32))
        centred_scaled_input, input_inverse_deviation = apply_layer_norm(mixed_product)
        normed_update = (centred_scaled_input * layer_norm_gains[1][:, None]).astype(jnp.bfloat16)
        update = channel_map(w_out[1], normed_update)
        gate = jax.nn.sigmoid(channel_map(w_out[0], zn))
        cot = cot_one.astype(jnp.float32)
        d_gate = (cot * update * gate * (1.0 - gate)).astype(jnp.bfloat16)
        d_update = (cot * gate).astype(jnp.bfloat16)
        normed_update_gradient = channel_back(w_out[1], d_update)
        mixed_gradient = layer_norm_backward(normed_update_gradient * layer_norm_gains[1][:, None], centred_scaled_input, input_inverse_deviation).astype(jnp.bfloat16)
        d_left = jnp.einsum('icj,jck->ick', mixed_gradient.astype(jnp.float32), right.astype(jnp.float32))
        d_right = jnp.einsum('icj,ick->jck', mixed_gradient.astype(jnp.float32), left.astype(jnp.float32))
        grads = gating_back(d_left, pre[0], pre[1], mask) + gating_back(d_right, pre[2], pre[3], mask)
        grad_proj = jnp.stack([weight_grad(zn, grads[p]) for p in range(4)])
        grad_out = jnp.stack([weight_grad(zn, d_gate), weight_grad(normed_update, d_update)])
        normed_input_gradient = channel_back(w_out[0], d_gate)
        for p in range(4):
            normed_input_gradient = normed_input_gradient + channel_back(w_proj[p], grads[p])
        norm_gain_gradients = jnp.stack([lax.optimization_barrier(jnp.sum(normed_input_gradient * normed_values, axis=(0, 2))), lax.optimization_barrier(jnp.sum(normed_input_gradient, axis=(0, 2))), lax.optimization_barrier(jnp.sum(normed_update_gradient * centred_scaled_input, axis=(0, 2)))])
        pair_grad = layer_norm_backward(normed_input_gradient * layer_norm_gains[0][:, None], normed_values, rstd).astype(jnp.bfloat16)
        return (pair_grad, grad_proj, grad_out, norm_gain_gradients)
    results = lax.map(one_template, (pair, cotangent, coverage))
    scale = 1.0 / N
    return (results[0], lax.optimization_barrier(jnp.sum(results[1], axis=0)) * scale, lax.optimization_barrier(jnp.sum(results[2], axis=0)) * scale, lax.optimization_barrier(jnp.sum(results[3], axis=0)) * scale)
```

```python
import functools

import jax
import jax.numpy as jnp
from jax import lax
from jax.experimental import pallas as pl
from jax.experimental.pallas import tpu as pltpu
from jax.sharding import PartitionSpec as P

EPS = 1e-05
LANES = 128
PACK_ROWS = 256
F32 = jnp.float32
BF16 = jnp.bfloat16


def dot(a, b):
    return jnp.dot(a, b, preferred_element_type=F32)


def dot_nt(a, b):
    return lax.dot_general(a, b, (((1,), (1,)), ((), ())), preferred_element_type=F32)


def dot_tn(a, b):
    return lax.dot_general(a, b, (((0,), (0,)), ((), ())), preferred_element_type=F32)


def transposed(weight):
    return weight.astype(F32).T.astype(BF16)


def column(row):
    n = row.shape[1]
    eye = lax.broadcasted_iota(jnp.int32, (n, n), 0) == lax.broadcasted_iota(jnp.int32, (n, n), 1)
    return jnp.sum(jnp.where(eye, row, 0.0), axis=1, keepdims=True)


def as_row(col):
    n = col.shape[0]
    eye = lax.broadcasted_iota(jnp.int32, (n, n), 0) == lax.broadcasted_iota(jnp.int32, (n, n), 1)
    return jnp.sum(jnp.where(eye, col, 0.0), axis=0, keepdims=True)


def layer_norm(x):
    mean = jnp.mean(x, axis=0, keepdims=True)
    centred = x - mean
    rstd = lax.rsqrt(jnp.mean(centred * centred, axis=0, keepdims=True) + EPS)
    return centred * rstd, rstd


def mask_rows(first_ref, tokens_ref, cover_ref, column_mask, templ, rows):
    width, tiles = tokens_ref.shape[0], cover_ref.shape[1]
    tile = width // tiles
    block = pl.program_id(0) * LANES // tile
    out = []
    for t in range(templ):
        for r in range(rows):
            i = first_ref[0] + r
            scalar = tokens_ref[i] * cover_ref[t, i // tile, block]
            out.append(column_mask * scalar.astype(F32))
    return out


def project_kernel(templ, rows, first_ref, tokens_ref, cover_ref, pair_ref, tok_ref, w_ref, gains_ref, bias_ref, lr_ref, zn_ref, left_scr, right_scr):
    count, chans = templ * rows, pair_ref.shape[1]
    gain, bias = column(gains_ref[0:1, :]), column(bias_ref[...])
    masks = mask_rows(first_ref, tokens_ref, cover_ref, tok_ref[...].astype(F32), templ, rows)
    weights = jnp.concatenate([transposed(w_ref[p]) for p in range(4)], axis=0)
    for pos in range(0, count, 2):
        zn = []
        for q in (pos, pos + 1):
            normed, _ = layer_norm(pair_ref[q].astype(F32))
            zn.append((normed * gain + bias).astype(BF16))
        zn = jnp.concatenate(zn, axis=1)
        zn_ref[0, :, pos * LANES:(pos + 2) * LANES] = zn
        pre = dot(weights, zn)
        for j in range(2):
            part = pre[:, j * LANES:(j + 1) * LANES]
            pre_p = [part[p * chans:(p + 1) * chans] for p in range(4)]
            mask = masks[pos + j]
            where = pl.ds(pos + j, chans, stride=count)
            left_scr[where, :] = jax.nn.sigmoid(pre_p[0]) * pre_p[1] * mask
            right_scr[where, :] = jax.nn.sigmoid(pre_p[2]) * pre_p[3] * mask
    groups, _, per, _, _ = lr_ref.shape
    lr_ref[:, 0] = left_scr[...].astype(BF16).reshape(groups, per, count, LANES)
    lr_ref[:, 1] = right_scr[...].astype(BF16).reshape(groups, per, count, LANES)


def prepare_kernel(templ, rows, first_ref, tokens_ref, cover_ref, pair_ref, cot_ref, zn_ref, tok_ref, w_ref, wo_ref, fac_ref, cg_ref, du_ref, normed_ref, rstd_ref, dout_ref, scr):
    count, chans = templ * rows, pair_ref.shape[1]
    masks = mask_rows(first_ref, tokens_ref, cover_ref, tok_ref[...].astype(F32), templ, rows)
    weights = jnp.concatenate([transposed(w_ref[p]) for p in range(4)] + [transposed(wo_ref[0])], axis=0)
    w_back = wo_ref[1]
    for pos in range(0, count, 2):
        span = slice(pos * LANES, (pos + 2) * LANES)
        pre = dot(weights, zn_ref[0, :, span])
        mask = jnp.concatenate([masks[pos], masks[pos + 1]], axis=1)
        pre_p = [pre[p * chans:(p + 1) * chans] for p in range(5)]
        for p in (0, 2):
            sig = jax.nn.sigmoid(pre_p[p])
            sm = sig * mask
            fac_ref[0, p * chans:(p + 1) * chans, span] = sm * pre_p[p + 1] * (1.0 - sig)
            fac_ref[0, (p + 1) * chans:(p + 2) * chans, span] = sm
        gate = jax.nn.sigmoid(pre_p[4])
        cot = jnp.concatenate([cot_ref[pos], cot_ref[pos + 1]], axis=1).astype(F32)
        d_update = cot * gate
        cg_ref[0, :, span] = d_update * (1.0 - gate)
        d_update = d_update.astype(BF16)
        du_ref[0, :, span] = d_update
        d_outn = dot(w_back, d_update)
        for j in range(2):
            scr[pl.ds(pos + j, chans, stride=count), :] = d_outn[:, j * LANES:(j + 1) * LANES]
            normed, rstd = layer_norm(pair_ref[pos + j].astype(F32))
            lanes = slice((pos + j) * LANES, (pos + j + 1) * LANES)
            normed_ref[0, :, lanes] = normed
            rstd_ref[0, :, lanes] = rstd
    dout_ref[...] = scr[...].reshape(chans, count, LANES)


def mixed_kernel(rows, cols_ref, mixed_ref, left_ref, right_ref):
    n, _, per, count, width = cols_ref.shape
    templ = count // rows
    for c in range(per):
        left_all = cols_ref[:, 0, c].astype(F32)
        right_all = cols_ref[:, 1, c].astype(F32)
        parts = []
        for t in range(templ):
            left = left_all[:, t * rows:(t + 1) * rows].reshape(n * rows, width).astype(BF16)
            right = right_all[:, t * rows:(t + 1) * rows].reshape(n * rows, width).astype(BF16)
            left_ref[c * templ + t] = left
            right_ref[c * templ + t] = right
            parts.append(dot_nt(left, right).reshape(n, rows, width))
        mixed_ref[:, c] = jnp.concatenate(parts, axis=1).astype(BF16)


def triangle_back_kernel(rows, dmix_ref, left_ref, right_ref, out_ref):
    n, per, count, width = dmix_ref.shape
    templ = count // rows
    for c in range(per):
        dmix_all = dmix_ref[:, c].astype(F32)
        left_parts, right_parts = [], []
        for t in range(templ):
            dmix = dmix_all[:, t * rows:(t + 1) * rows].reshape(n * rows, width).astype(BF16)
            left_parts.append(dot(dmix, right_ref[c * templ + t]).reshape(n, rows, width))
            right_parts.append(dot_tn(dmix, left_ref[c * templ + t]).reshape(n, rows, width))
        out_ref[:, 0, c] = jnp.concatenate(left_parts, axis=1).astype(BF16)
        out_ref[:, 1, c] = jnp.concatenate(right_parts, axis=1).astype(BF16)


def tree_sum(parts):
    while len(parts) > 1:
        parts = [a + b for a, b in zip(parts[::2], parts[1::2])] + parts[len(parts) // 2 * 2:]
    return parts[0]


def channel_sum(chans, value):
    accs = [None] * 4
    for c in range(chans):
        v = value(c)
        accs[c % 4] = v if accs[c % 4] is None else accs[c % 4] + v
    return tree_sum([a for a in accs if a is not None])


def mixed_norm_back_kernel(gains_ref, mixed_ref, dout_ref, dmix_ref):
    chans = mixed_ref.shape[0]
    inv = 1.0 / chans
    mean = channel_sum(chans, lambda c: mixed_ref[c].astype(F32)) * inv
    mean_h = channel_sum(chans, lambda c: dout_ref[c] * gains_ref[1, c]) * inv

    def squares(c):
        centred = mixed_ref[c].astype(F32) - mean
        return centred * centred

    rstd = lax.rsqrt(channel_sum(chans, squares) * inv + EPS)

    def products(c):
        return dout_ref[c] * gains_ref[1, c] * ((mixed_ref[c].astype(F32) - mean) * rstd)

    mean_p = channel_sum(chans, products) * inv
    for c in range(chans):
        xhat = (mixed_ref[c].astype(F32) - mean) * rstd
        dmix_ref[c] = (rstd * (dout_ref[c] * gains_ref[1, c] - mean_h - xhat * mean_p)).astype(BF16)


def update_kernel(gains_ref, mixed_ref, dout_ref, zn_ref, cg_ref, du_ref, wo_ref, dgate_ref, grads_ref, scr, norm_scr, outn_scr):
    chans, count, _ = mixed_ref.shape
    inv = 1.0 / chans
    mean = channel_sum(chans, lambda c: mixed_ref[c].astype(F32)) * inv

    def squares(c):
        centred = mixed_ref[c].astype(F32) - mean
        return centred * centred

    rstd = lax.rsqrt(channel_sum(chans, squares) * inv + EPS)
    for c in range(chans):
        xhat = (mixed_ref[c].astype(F32) - mean) * rstd
        scr[c * count:(c + 1) * count, :] = xhat * gains_ref[1, c]
        norm_scr[c:c + 1, :] = jnp.sum(dout_ref[c] * xhat, axis=0, keepdims=True)
    w_update = transposed(wo_ref[1])
    for pos in range(count):
        span = slice(pos * LANES, (pos + 1) * LANES)
        outn_scr[:, span] = scr[pl.ds(pos, chans, stride=count), :].astype(BF16)
    update = dot(w_update, outn_scr[...])
    d_gate = (cg_ref[0] * update).astype(BF16)
    dgate_ref[0] = d_gate
    gate_grad = dot_nt(zn_ref[0], d_gate)
    out_grad = dot_nt(outn_scr[...], du_ref[0])
    norm = as_row(jnp.sum(norm_scr[...], axis=1, keepdims=True))

    @pl.when(pl.program_id(0) == 0)
    def _():
        grads_ref[...] = jnp.zeros_like(grads_ref)

    grads_ref[0:chans, 0:chans] += gate_grad
    grads_ref[0:chans, chans:2 * chans] += out_grad
    grads_ref[chans:chans + 1, 0:chans] += norm


def gating_back_kernel(dlr_ref, fac_ref, zn_ref, dgate_ref, normed_ref, w_ref, wo_ref, pre_grads_ref, dzn_ref, pack_ref, left_scr, right_scr, d_scr):
    groups, _, per, count, _ = dlr_ref.shape
    chans = groups * per
    left_scr[...] = dlr_ref[:, 0].astype(F32).reshape(chans * count, LANES)
    right_scr[...] = dlr_ref[:, 1].astype(F32).reshape(chans * count, LANES)
    d_scr[4 * chans:5 * chans, :] = dgate_ref[0]
    for pos in range(count):
        span = slice(pos * LANES, (pos + 1) * LANES)
        where = pl.ds(pos, chans, stride=count)
        d_left, d_right = left_scr[where, :], right_scr[where, :]
        for p in range(4):
            d = d_left if p < 2 else d_right
            d_scr[p * chans:(p + 1) * chans, span] = (d * fac_ref[0, p * chans:(p + 1) * chans, span]).astype(BF16)
    weights = jnp.concatenate([w_ref[0], w_ref[1], w_ref[2], w_ref[3], wo_ref[0]], axis=1)
    d_zn = dot(weights, d_scr[...])
    dzn_ref[0] = d_zn
    grads = dot_nt(zn_ref[0], d_scr[0:4 * chans, :])
    bias_grad = as_row(jnp.sum(d_zn, axis=1, keepdims=True))
    gain_grad = as_row(jnp.sum(d_zn * normed_ref[0], axis=1, keepdims=True))

    @pl.when(pl.program_id(0) == 0)
    def _():
        pack_ref[...] = jnp.zeros_like(pack_ref)
        pack_ref[2 * chans:3 * chans, :] = pre_grads_ref[0:chans, :]
        pack_ref[3 * chans:3 * chans + 1, :] = pre_grads_ref[chans:chans + 1, :]

    pack_ref[0:chans, :] += grads[:, 0:2 * chans]
    pack_ref[chans:2 * chans, :] += grads[:, 2 * chans:4 * chans]
    pack_ref[3 * chans + 1:3 * chans + 2, 0:chans] += gain_grad
    pack_ref[3 * chans + 2:3 * chans + 3, 0:chans] += bias_grad


def pair_grad_kernel(dzn_ref, normed_ref, rstd_ref, gains_ref, out_ref):
    gain = column(gains_ref[0:1, :])
    for pos in range(out_ref.shape[0]):
        span = slice(pos * LANES, (pos + 1) * LANES)
        h = dzn_ref[0, :, span] * gain
        normed = normed_ref[0, :, span]
        mean_h = jnp.mean(h, axis=0, keepdims=True)
        mean_p = jnp.mean(h * normed, axis=0, keepdims=True)
        out_ref[pos] = (rstd_ref[0, :, span] * (h - mean_h - normed * mean_p)).astype(BF16)


def unpack_kernel(scale, pack_ref, proj_ref, out_ref, norm_ref):
    chans = proj_ref.shape[1]
    for p in range(4):
        proj_ref[p] = pack_ref[(p // 2) * chans:(p // 2 + 1) * chans, (p % 2) * chans:(p % 2 + 1) * chans] * scale
    for p in range(2):
        out_ref[p] = pack_ref[2 * chans:3 * chans, p * chans:(p + 1) * chans] * scale
    for row, place in ((0, 1), (1, 2), (2, 0)):
        norm_ref[row:row + 1, :] = pack_ref[3 * chans + place:3 * chans + place + 1, 0:chans] * scale


def exchange(x):
    return lax.all_to_all(x, "row", split_axis=0, concat_axis=0, tiled=True)


def full(shape):
    return pl.BlockSpec(shape, lambda b: (0,) * len(shape))


SMEM = pl.BlockSpec(memory_space=pltpu.SMEM)


def params():
    return pltpu.CompilerParams(vmem_limit_bytes=40 * 1024 * 1024)


def per_device(n, pair, cotangent, token_mask, coverage, w_proj, w_out, layer_norm_gains, ln_bias):
    templ, rows, chans, width = pair.shape
    count = templ * rows
    blocks = width // LANES
    direct = chans % n == 0
    groups = n if direct else chans
    per = chans // groups
    lanes = count * LANES
    first = (lax.axis_index("row") * rows).astype(jnp.int32).reshape(1)
    pair_rows = pair.reshape(count, chans, width)
    cot_rows = cotangent.reshape(count, chans, width)
    tokens_row = token_mask.reshape(1, width)
    bias_row = ln_bias.reshape(1, chans)

    rows_spec = pl.BlockSpec((count, chans, LANES), lambda b: (0, 0, b))
    tok_spec = pl.BlockSpec((1, LANES), lambda b: (0, b))
    lr_spec = pl.BlockSpec((groups, 2, per, count, LANES), lambda b: (0, 0, 0, 0, b))
    cat_spec = pl.BlockSpec((1, chans, lanes), lambda b: (b, 0, 0))
    fac_spec = pl.BlockSpec((1, 4 * chans, lanes), lambda b: (b, 0, 0))
    one_spec = pl.BlockSpec((1, 1, lanes), lambda b: (b, 0, 0))
    chan_spec = pl.BlockSpec((chans, count, LANES), lambda b: (0, 0, b))
    w_spec, wo_spec, gains_spec = full(w_proj.shape), full(w_out.shape), full(layer_norm_gains.shape)
    scratch = pltpu.VMEM((chans * count, LANES), F32)
    cat = lambda dtype: jax.ShapeDtypeStruct((blocks, chans, lanes), dtype)
    by_chan = lambda dtype: jax.ShapeDtypeStruct((chans, count, width), dtype)

    lr, zn = pl.pallas_call(
        functools.partial(project_kernel, templ, rows),
        grid=(blocks,),
        in_specs=[SMEM, SMEM, SMEM, rows_spec, tok_spec, w_spec, gains_spec, full(bias_row.shape)],
        out_specs=[lr_spec, cat_spec],
        out_shape=[jax.ShapeDtypeStruct((groups, 2, per, count, width), BF16), cat(BF16)],
        scratch_shapes=[scratch, scratch],
        compiler_params=params(),
        name="project",
    )(first, token_mask, coverage, pair_rows, tokens_row, w_proj, layer_norm_gains, bias_row)

    fac, cg, d_update, normed, rstd, d_outn = pl.pallas_call(
        functools.partial(prepare_kernel, templ, rows),
        grid=(blocks,),
        in_specs=[SMEM, SMEM, SMEM, rows_spec, rows_spec, cat_spec, tok_spec, w_spec, wo_spec],
        out_specs=[fac_spec, cat_spec, cat_spec, cat_spec, one_spec, chan_spec],
        out_shape=[
            jax.ShapeDtypeStruct((blocks, 4 * chans, lanes), F32),
            cat(F32),
            cat(BF16),
            cat(F32),
            jax.ShapeDtypeStruct((blocks, 1, lanes), F32),
            by_chan(F32),
        ],
        scratch_shapes=[scratch],
        compiler_params=params(),
        name="prepare",
    )(first, token_mask, coverage, pair_rows, cot_rows, zn, tokens_row, w_proj, w_out)

    if direct:
        cols = exchange(lr)
        mixed, left_cols, right_cols = pl.pallas_call(
            functools.partial(mixed_kernel, rows),
            out_shape=[
                jax.ShapeDtypeStruct((n, per, count, width), BF16),
                jax.ShapeDtypeStruct((per * templ, width, width), BF16),
                jax.ShapeDtypeStruct((per * templ, width, width), BF16),
            ],
            compiler_params=params(),
            name="mixed",
        )(cols)
        mixed_rows = exchange(mixed).reshape(chans, count, width)
    else:
        slices = chans * templ // n
        cols = lr.reshape(chans, 2, templ, rows, width).transpose(0, 2, 1, 3, 4)
        cols = exchange(cols.reshape(n * slices, 2, rows, width)).reshape(n, slices, 2, rows, width)
        left_cols, right_cols = cols.transpose(2, 1, 0, 3, 4).reshape(2, slices, width, width)
        mixed = jnp.einsum("sik,sjk->sij", left_cols, right_cols, preferred_element_type=F32)
        mixed = mixed.astype(BF16).reshape(slices, n, rows, width).transpose(1, 0, 2, 3)
        mixed_rows = exchange(mixed.reshape(n * slices, rows, width)).reshape(chans, count, width)

    d_mixed = pl.pallas_call(
        mixed_norm_back_kernel,
        grid=(blocks,),
        in_specs=[SMEM, chan_spec, chan_spec],
        out_specs=chan_spec,
        out_shape=by_chan(BF16),
        compiler_params=params(),
        name="mixed_norm_back",
    )(layer_norm_gains, mixed_rows, d_outn)

    d_gate, out_grads = pl.pallas_call(
        update_kernel,
        grid=(blocks,),
        in_specs=[SMEM, chan_spec, chan_spec, cat_spec, cat_spec, cat_spec, wo_spec],
        out_specs=[cat_spec, full((chans + 8, 2 * chans))],
        out_shape=[cat(BF16), jax.ShapeDtypeStruct((chans + 8, 2 * chans), F32)],
        scratch_shapes=[scratch, pltpu.VMEM((chans, LANES), F32), pltpu.VMEM((chans, lanes), BF16)],
        compiler_params=params(),
        name="update",
    )(layer_norm_gains, mixed_rows, d_outn, zn, cg, d_update, w_out)

    if direct:
        dmix_cols = exchange(d_mixed.reshape(n, per, count, width))
        d_lr = pl.pallas_call(
            functools.partial(triangle_back_kernel, rows),
            out_shape=jax.ShapeDtypeStruct((n, 2, per, count, width), BF16),
            compiler_params=params(),
            name="triangle_back",
        )(dmix_cols, left_cols, right_cols)
        d_lr = exchange(d_lr)
    else:
        dmix_cols = exchange(d_mixed.reshape(n * slices, rows, width)).reshape(n, slices, rows, width)
        dmix_cols = dmix_cols.transpose(1, 0, 2, 3).reshape(slices, width, width)
        d_left = jnp.einsum("sij,sjk->sik", dmix_cols, right_cols, preferred_element_type=F32)
        d_right = jnp.einsum("sij,sik->sjk", dmix_cols, left_cols, preferred_element_type=F32)
        d_lr = jnp.stack([d_left.astype(BF16), d_right.astype(BF16)]).reshape(2, slices, n, rows, width)
        d_lr = exchange(d_lr.transpose(2, 1, 0, 3, 4).reshape(n * slices, 2, rows, width))
        d_lr = d_lr.reshape(chans, templ, 2, rows, width).transpose(0, 2, 1, 3, 4)
        d_lr = d_lr.reshape(groups, 2, per, count, width)

    d_zn, pack = pl.pallas_call(
        gating_back_kernel,
        grid=(blocks,),
        in_specs=[lr_spec, fac_spec, cat_spec, cat_spec, cat_spec, w_spec, wo_spec, full((chans + 8, 2 * chans))],
        out_specs=[cat_spec, full((PACK_ROWS, 2 * chans))],
        out_shape=[cat(F32), jax.ShapeDtypeStruct((PACK_ROWS, 2 * chans), F32)],
        scratch_shapes=[scratch, scratch, pltpu.VMEM((5 * chans, lanes), BF16)],
        compiler_params=params(),
        name="gating_back",
    )(d_lr, fac, zn, d_gate, normed, w_proj, w_out, out_grads)

    pair_grad = pl.pallas_call(
        pair_grad_kernel,
        grid=(blocks,),
        in_specs=[cat_spec, cat_spec, one_spec, gains_spec],
        out_specs=rows_spec,
        out_shape=jax.ShapeDtypeStruct((count, chans, width), BF16),
        compiler_params=params(),
        name="pair_grad",
    )(d_zn, normed, rstd, layer_norm_gains)

    share = PACK_ROWS // n
    mine = exchange(pack).reshape(n, share, 2 * chans).sum(axis=0)
    total = exchange(jnp.broadcast_to(mine[None], (n, share, 2 * chans)).reshape(PACK_ROWS, 2 * chans))
    grad_proj, grad_out, norm_grads = pl.pallas_call(
        functools.partial(unpack_kernel, 1.0 / width),
        out_shape=[
            jax.ShapeDtypeStruct(w_proj.shape, F32),
            jax.ShapeDtypeStruct(w_out.shape, F32),
            jax.ShapeDtypeStruct((3, chans), F32),
        ],
        name="unpack",
    )(total)
    return pair_grad.reshape(pair.shape), grad_proj, grad_out, norm_grads


def solution(mesh):
    return jax.shard_map(
        functools.partial(per_device, mesh.shape["row"]),
        mesh=mesh,
        in_specs=(
            P("groups", "row", None, None),
            P("groups", "row", None, None),
            P("groups"),
            P("groups", None, None),
            P(),
            P(),
            P(),
            P(),
        ),
        out_specs=(
            P("groups", "row", None, None),
            P("groups", None, None),
            P("groups", None, None),
            P("groups", None),
        ),
        check_vma=False,
    )
```

```python
import functools

import jax
import jax.numpy as jnp
from jax import lax
from jax.experimental import pallas as pl
from jax.experimental.pallas import tpu as pltpu
from jax.sharding import PartitionSpec as P

EPS = 1e-05
LANES = 128
F32 = jnp.float32
BF16 = jnp.bfloat16


def dot(a, b):
    return jnp.dot(a, b, preferred_element_type=F32)


def dot_nt(a, b):
    return lax.dot_general(a, b, (((1,), (1,)), ((), ())), preferred_element_type=F32)


def dot_tn(a, b):
    return lax.dot_general(a, b, (((0,), (0,)), ((), ())), preferred_element_type=F32)


def transposed(weight):
    return weight.astype(F32).T.astype(BF16)


def column(row):
    n = row.shape[1]
    eye = lax.broadcasted_iota(jnp.int32, (n, n), 0) == lax.broadcasted_iota(jnp.int32, (n, n), 1)
    return jnp.sum(jnp.where(eye, row, 0.0), axis=1, keepdims=True)


def as_row(col):
    n = col.shape[0]
    eye = lax.broadcasted_iota(jnp.int32, (n, n), 0) == lax.broadcasted_iota(jnp.int32, (n, n), 1)
    return jnp.sum(jnp.where(eye, col, 0.0), axis=0, keepdims=True)


def layer_norm(x):
    mean = jnp.mean(x, axis=0, keepdims=True)
    centred = x - mean
    rstd = lax.rsqrt(jnp.mean(centred * centred, axis=0, keepdims=True) + EPS)
    return centred * rstd, rstd


def mask_rows(me_ref, tokens_ref, cover_ref, tok_ref, block, rows):
    width, (tiles, _, templ) = tokens_ref.shape[1], cover_ref.shape
    tile = width // tiles
    first = me_ref[0] * rows
    here = lax.broadcasted_iota(jnp.int32, (rows, width), 0) + first == lax.broadcasted_iota(jnp.int32, (rows, width), 1)
    row_mask = jnp.sum(jnp.where(here, tokens_ref[...].astype(F32), 0.0), axis=1, keepdims=True)
    column_mask = tok_ref[...].astype(F32)
    cover = cover_ref[first // tile].astype(F32)
    here = lax.broadcasted_iota(jnp.int32, (tiles, templ), 0) == block() * LANES // tile
    cover = jnp.sum(jnp.where(here, cover, 0.0), axis=0, keepdims=True)
    out = []
    for t in range(templ):
        masked = column_mask * cover[:, t:t + 1]
        out += [masked * row_mask[r:r + 1, :] for r in range(rows)]
    return out


def front_kernel(rows, block, me_ref, tokens_ref, cover_ref, pair_ref, cot_ref, tok_ref, w_ref, wo_ref, gains_ref, bias_ref, lr_ref, zn_ref, fac_ref, cg_ref, du_ref, normed_ref, rstd_ref, dout_ref, wcat_ref, left_scr, right_scr, dout_scr):
    count, chans, _ = pair_ref.shape
    wcat_ref[...] = jnp.concatenate([w_ref[0], w_ref[1], w_ref[2], w_ref[3], wo_ref[0]], axis=1)
    gain, bias = column(gains_ref[0:1, :]), column(bias_ref[...])
    masks = mask_rows(me_ref, tokens_ref, cover_ref, tok_ref, block, rows)
    weights = jnp.concatenate([transposed(w_ref[p]) for p in range(4)] + [transposed(wo_ref[0])], axis=0)
    w_back = wo_ref[1]
    for pos in range(0, count, 2):
        span = slice(pos * LANES, (pos + 2) * LANES)
        zn = []
        for q in (pos, pos + 1):
            normed, rstd = layer_norm(pair_ref[q].astype(F32))
            lanes = slice(q * LANES, (q + 1) * LANES)
            normed_ref[0, :, lanes] = normed
            rstd_ref[0, :, lanes] = rstd
            zn.append((normed * gain + bias).astype(BF16))
        zn = jnp.concatenate(zn, axis=1)
        zn_ref[0, :, span] = zn
        pre = dot(weights, zn)
        for j in range(2):
            part = pre[:, j * LANES:(j + 1) * LANES]
            pre_p = [part[p * chans:(p + 1) * chans] for p in range(5)]
            mask = masks[pos + j]
            where = pl.ds(pos + j, chans, stride=count)
            lanes = slice((pos + j) * LANES, (pos + j + 1) * LANES)
            for p, scr in ((0, left_scr), (2, right_scr)):
                sig = jax.nn.sigmoid(pre_p[p])
                sig_mask = sig * mask
                both = sig_mask * pre_p[p + 1]
                scr[where, :] = both
                fac_ref[0, p * chans:(p + 1) * chans, lanes] = both * (1.0 - sig)
                fac_ref[0, (p + 1) * chans:(p + 2) * chans, lanes] = sig_mask
            gate = jax.nn.sigmoid(pre_p[4])
            d_update = cot_ref[pos + j].astype(F32) * gate
            cg_ref[0, :, lanes] = d_update * (1.0 - gate)
            du_ref[0, :, lanes] = d_update.astype(BF16)
        d_outn = dot(w_back, du_ref[0, :, span])
        for j in range(2):
            dout_scr[pl.ds(pos + j, chans, stride=count), :] = d_outn[:, j * LANES:(j + 1) * LANES]
    groups, both, _, _ = lr_ref.shape
    per = both // 2
    lr_ref[:, 0:per] = left_scr[...].astype(BF16).reshape(groups, per, count, LANES)
    lr_ref[:, per:both] = right_scr[...].astype(BF16).reshape(groups, per, count, LANES)
    dout_ref[...] = dout_scr[...].reshape(chans, count, LANES)


def mixed_kernel(rows, cols_ref, mixed_ref, left_ref, right_ref):
    n, both, count, width = cols_ref.shape
    per, templ = both // 2, count // rows
    for c in range(per):
        left_all = cols_ref[:, c].astype(F32)
        right_all = cols_ref[:, per + c].astype(F32)
        parts = []
        for t in range(templ):
            left = left_all[:, t * rows:(t + 1) * rows].reshape(n * rows, width).astype(BF16)
            right = right_all[:, t * rows:(t + 1) * rows].reshape(n * rows, width).astype(BF16)
            left_ref[c * templ + t] = left
            right_ref[c * templ + t] = right
            parts.append(dot_nt(left, right).reshape(n, rows, width))
        mixed_ref[:, c] = jnp.concatenate(parts, axis=1).astype(BF16)


def triangle_back_kernel(rows, dmix_ref, left_ref, right_ref, extra_ref, out_ref):
    n, per, count, width = dmix_ref.shape
    templ = count // rows
    for c in range(per):
        dmix_all = dmix_ref[:, c].astype(F32)
        left_parts, right_parts = [], []
        for t in range(templ):
            dmix = dmix_all[:, t * rows:(t + 1) * rows].reshape(n * rows, width).astype(BF16)
            left_parts.append(dot(dmix, right_ref[c * templ + t]).reshape(n, rows, width))
            right_parts.append(dot_tn(dmix, left_ref[c * templ + t]).reshape(n, rows, width))
        out_ref[:, c] = jnp.concatenate(left_parts, axis=1).astype(BF16)
        out_ref[:, per + c] = jnp.concatenate(right_parts, axis=1).astype(BF16)
    out_ref[:, 2 * per] = extra_ref[...]


def split(x):
    high = x.astype(BF16).astype(F32)
    return high, x - high


def tree_sum(parts):
    while len(parts) > 1:
        parts = [a + b for a, b in zip(parts[::2], parts[1::2])] + parts[len(parts) // 2 * 2:]
    return parts[0]


def channel_sum(chans, value):
    accs = [None] * 4
    for c in range(chans):
        v = value(c)
        accs[c % 4] = v if accs[c % 4] is None else accs[c % 4] + v
    return tree_sum([a for a in accs if a is not None])


def middle_kernel(n, block, gains_ref, mixed_ref, dout_ref, zn_ref, cg_ref, du_ref, wo_ref, dmix_ref, dgate_ref, grads_ref, scr, norm_scr, outn_scr):
    chans, count, _ = mixed_ref.shape
    inv = 1.0 / chans
    mean = channel_sum(chans, lambda c: mixed_ref[c].astype(F32)) * inv
    mean_h = channel_sum(chans, lambda c: dout_ref[c] * gains_ref[1, c]) * inv

    def squares(c):
        centred = mixed_ref[c].astype(F32) - mean
        return centred * centred

    rstd = lax.rsqrt(channel_sum(chans, squares) * inv + EPS)

    def products(c):
        gain = gains_ref[1, c]
        xhat = (mixed_ref[c].astype(F32) - mean) * rstd
        outn = xhat * gain
        scr[c * count:(c + 1) * count, :] = outn
        product = dout_ref[c] * xhat
        norm_scr[c:c + 1, :] = jnp.sum(product, axis=0, keepdims=True)
        return product * gain

    mean_p = channel_sum(chans, products) * inv
    for c in range(chans):
        xhat = (mixed_ref[c].astype(F32) - mean) * rstd
        dmix_ref[c] = (rstd * (dout_ref[c] * gains_ref[1, c] - mean_h - xhat * mean_p)).astype(BF16)
    w_update = transposed(wo_ref[1])
    for pos in range(count):
        span = slice(pos * LANES, (pos + 1) * LANES)
        outn_scr[:, span] = scr[pl.ds(pos, chans, stride=count), :].astype(BF16)
    update = dot(w_update, outn_scr[...])
    d_gate = (cg_ref[0] * update).astype(BF16)
    dgate_ref[0] = d_gate
    gate_grad = dot_nt(zn_ref[0], d_gate)
    out_grad = dot_nt(outn_scr[...], du_ref[0])
    norm = as_row(jnp.sum(norm_scr[...], axis=1, keepdims=True))
    if n:
        grads = jnp.concatenate([gate_grad, out_grad], axis=1)
        norm = jnp.concatenate([norm, jnp.zeros_like(norm)], axis=1)
        high, low = split(grads)
        norm_high, norm_low = split(norm)
        share = chans // n
        pad = [jnp.zeros((4 - share, 2 * chans), F32)] if share < 4 else []
        rest = jnp.zeros((6, 2 * chans), F32)
        for d in range(n):
            mine = slice(d * share, (d + 1) * share)
            tile = jnp.concatenate([norm_high, norm_low, high[mine], *pad, low[mine], *pad, rest], axis=0)
            grads_ref[d] = tile.astype(BF16)
        return

    @pl.when(block() == 0)
    def _():
        grads_ref[...] = jnp.zeros_like(grads_ref)

    grads_ref[0:chans, 0:chans] += gate_grad
    grads_ref[0:chans, chans:2 * chans] += out_grad
    grads_ref[chans:chans + 1, 0:chans] += norm


def back_kernel(blocks, block, me_ref, dlr_ref, fac_ref, zn_ref, dgate_ref, normed_ref, rstd_ref, wcat_ref, gains_ref, pair_ref, keep_ref, send_ref, done_ref, left_scr, right_scr, d_scr, pack_scr):
    groups, parts, count, _ = dlr_ref.shape
    per = parts // 2
    chans = groups * per
    left_scr[...] = dlr_ref[:, 0:per].astype(F32).reshape(chans * count, LANES)
    right_scr[...] = dlr_ref[:, per:2 * per].astype(F32).reshape(chans * count, LANES)
    d_scr[4 * chans:5 * chans, :] = dgate_ref[0]
    for pos in range(count):
        span = slice(pos * LANES, (pos + 1) * LANES)
        where = pl.ds(pos, chans, stride=count)
        d_left, d_right = left_scr[where, :], right_scr[where, :]
        for p in range(4):
            d = d_left if p < 2 else d_right
            d_scr[p * chans:(p + 1) * chans, span] = (d * fac_ref[0, p * chans:(p + 1) * chans, span]).astype(BF16)
    d_zn = dot(wcat_ref[...], d_scr[...])
    gain = column(gains_ref[0:1, :])
    for pos in range(count):
        span = slice(pos * LANES, (pos + 1) * LANES)
        h = d_zn[:, span] * gain
        normed = normed_ref[0, :, span]
        mean_h = jnp.mean(h, axis=0, keepdims=True)
        mean_p = jnp.mean(h * normed, axis=0, keepdims=True)
        pair_ref[pos] = (rstd_ref[0, :, span] * (h - mean_h - normed * mean_p)).astype(BF16)
    grads = dot_nt(zn_ref[0], d_scr[0:4 * chans, :])
    bias_grad = as_row(jnp.sum(d_zn, axis=1, keepdims=True))
    gain_grad = as_row(jnp.sum(d_zn * normed_ref[0], axis=1, keepdims=True))

    @pl.when(block() == 0)
    def _():
        pack_scr[...] = jnp.zeros_like(pack_scr)

    pack_scr[0:chans, :] += grads[:, 0:2 * chans]
    pack_scr[chans:2 * chans, :] += grads[:, 2 * chans:4 * chans]
    pack_scr[2 * chans:2 * chans + 1, 0:chans] += gain_grad
    pack_scr[2 * chans + 1:2 * chans + 2, 0:chans] += bias_grad

    @pl.when(block() == blocks - 1)
    def _():
        half = me_ref[0] % 2
        own = pl.multiple_of(half * chans, 8)
        other = pl.multiple_of((1 - half) * chans, 8)
        keep_ref[0:chans, :] = pack_scr[pl.ds(own, chans), :]
        send_ref[0:chans, :] = pack_scr[pl.ds(other, chans), :]
        keep_ref[chans:chans + 8, :] = pack_scr[2 * chans:2 * chans + 8, :]
        send_ref[chans:chans + 8, :] = pack_scr[2 * chans:2 * chans + 8, :]
        if parts > 2 * per:
            done_ref[...] = jnp.sum(dlr_ref[:, 2 * per].astype(F32), axis=0)
        else:
            done_ref[...] = jnp.zeros_like(done_ref)


def combine_kernel(keep_ref, got_ref, done_ref, out_ref):
    rows = keep_ref.shape[0] - 8
    total = keep_ref[...] + got_ref[...]
    norm_high, norm_low = split(total[rows:rows + 2])
    done_high, done_low = split(done_ref[2:6, :] + done_ref[6:10, :])
    tile = jnp.concatenate([norm_high, norm_low, done_high, done_low, jnp.zeros((4, total.shape[1]), F32)], axis=0)
    block = jnp.concatenate([total[0:rows], tile], axis=0).astype(BF16)
    for d in range(out_ref.shape[0]):
        out_ref[d] = block


def unpack_kernel(scale, share, pack_ref, done_ref, proj_ref, out_ref, norm_ref):
    n, chans = pack_ref.shape[0], proj_ref.shape[1]
    for half in range(2):
        total = tree_sum([pack_ref[d, 0:chans, :].astype(F32) for d in range(half, n, 2)]) * scale
        proj_ref[2 * half] = total[:, 0:chans]
        proj_ref[2 * half + 1] = total[:, chans:2 * chans]
    tiles = [pack_ref[d, chans:chans + 16, :].astype(F32) for d in range(n)]
    norms = tree_sum(tiles[::2])
    norms = (norms[0:2] + norms[2:4]) * scale
    norm_ref[0:2, :] = norms[:, 0:chans]
    if share:
        norm_ref[2:3, :] = (done_ref[0:1, 0:chans] + done_ref[1:2, 0:chans]) * scale
        for d in range(n):
            rows = (tiles[d][4:4 + share] + tiles[d][8:8 + share]) * scale
            out_ref[0, d * share:(d + 1) * share] = rows[:, 0:chans]
            out_ref[1, d * share:(d + 1) * share] = rows[:, chans:2 * chans]
    else:
        norm_ref[2:3, :] = done_ref[chans:chans + 1, 0:chans] * scale
        for p in range(2):
            out_ref[p] = done_ref[0:chans, p * chans:(p + 1) * chans] * scale


def exchange(x):
    return lax.all_to_all(x, "row", split_axis=0, concat_axis=0, tiled=True)


def per_device(n, pair, cotangent, token_mask, coverage, w_proj, w_out, layer_norm_gains, ln_bias):
    templ, rows, chans, width = pair.shape
    count = templ * rows
    blocks = width // LANES
    direct = blocks == 1 and chans % n == 0 and chans // n <= 4
    groups = n if direct else chans
    per = chans // groups
    lanes = count * LANES
    me = lax.axis_index("row").astype(jnp.int32).reshape(1)
    tokens_row = token_mask.reshape(1, width)

    params = pltpu.CompilerParams(vmem_limit_bytes=(16 if blocks == 1 else 40) * 1024 * 1024)
    smem = pl.BlockSpec(memory_space=pltpu.SMEM)
    whole = pl.BlockSpec(memory_space=pltpu.VMEM)

    def block_spec(shape, index):
        return whole if blocks == 1 else pl.BlockSpec(shape, index)

    def full(shape):
        return block_spec(shape, lambda b: (0,) * len(shape))

    def array(shape, dtype):
        return pltpu.VMEM(shape, dtype) if blocks == 1 else jax.ShapeDtypeStruct(shape, dtype)

    def from_hbm(x):
        return pltpu.with_memory_space_constraint(x, pltpu.HBM)

    def call(name, kernel, args, in_specs, out_specs, out_shape, scratch_shapes=()):
        block = (lambda: 0) if blocks == 1 else (lambda: pl.program_id(0))
        kernel = functools.partial(kernel, block)
        return pl.pallas_call(
            kernel,
            grid=() if blocks == 1 else (blocks,),
            in_specs=in_specs,
            out_specs=out_specs,
            out_shape=out_shape,
            scratch_shapes=scratch_shapes,
            compiler_params=params,
            name=name,
        )(*args)

    rows_spec = block_spec((count, chans, LANES), lambda b: (0, 0, b))
    tok_spec = block_spec((1, LANES), lambda b: (0, b))
    lr_spec = block_spec((groups, 2 * per, count, LANES), lambda b: (0, 0, 0, b))
    cat_spec = block_spec((1, chans, lanes), lambda b: (b, 0, 0))
    fac_spec = block_spec((1, 4 * chans, lanes), lambda b: (b, 0, 0))
    one_spec = block_spec((1, 1, lanes), lambda b: (b, 0, 0))
    chan_spec = block_spec((chans, count, LANES), lambda b: (0, 0, b))
    w_spec, wo_spec, gains_spec = full(w_proj.shape), full(w_out.shape), full(layer_norm_gains.shape)
    scratch = pltpu.VMEM((chans * count, LANES), F32)
    pair_rows = from_hbm(pair.reshape(count, chans, width))
    cot_rows = from_hbm(cotangent.reshape(count, chans, width))
    w_proj_in, w_out_in, gains_in = from_hbm(w_proj), from_hbm(w_out), from_hbm(layer_norm_gains)
    tokens_in, cover_in = from_hbm(tokens_row), from_hbm(coverage.transpose(1, 2, 0))
    half_rows = chans + 8

    def cat(dtype):
        return array((blocks, chans, lanes), dtype)

    lr, zn, fac, cg, d_update, normed, rstd, d_outn, wcat = call(
        "front",
        functools.partial(front_kernel, rows),
        (me, tokens_in, cover_in, pair_rows, cot_rows, tokens_in, w_proj_in, w_out_in, gains_in, from_hbm(ln_bias.reshape(1, chans))),
        [smem, full((1, width)), full(cover_in.shape), rows_spec, rows_spec, tok_spec, w_spec, wo_spec, gains_spec, full((1, chans))],
        [lr_spec, cat_spec, fac_spec, cat_spec, cat_spec, cat_spec, one_spec, chan_spec, full((chans, 5 * chans))],
        [
            jax.ShapeDtypeStruct((groups, 2 * per, count, width), BF16),
            cat(BF16),
            array((blocks, 4 * chans, lanes), F32),
            cat(F32),
            cat(BF16),
            cat(F32),
            array((blocks, 1, lanes), F32),
            array((chans, count, width), F32),
            array((chans, 5 * chans), BF16),
        ],
        [scratch, scratch, scratch],
    )

    if direct:
        cols = exchange(lr)
        mixed, left_cols, right_cols = pl.pallas_call(
            functools.partial(mixed_kernel, rows),
            out_shape=[
                jax.ShapeDtypeStruct((n, per, count, width), BF16),
                array((per * templ, width, width), BF16),
                array((per * templ, width, width), BF16),
            ],
            compiler_params=params,
            name="mixed",
        )(cols)
        mixed_rows = exchange(mixed).reshape(chans, count, width)
    else:
        slices = chans * templ // n
        cols = lr.reshape(chans, 2, templ, rows, width).transpose(0, 2, 1, 3, 4)
        cols = exchange(cols.reshape(n * slices, 2, rows, width)).reshape(n, slices, 2, rows, width)
        left_cols, right_cols = cols.transpose(2, 1, 0, 3, 4).reshape(2, slices, width, width)
        mixed = jnp.einsum("sik,sjk->sij", left_cols, right_cols, preferred_element_type=F32)
        mixed = mixed.astype(BF16).reshape(slices, n, rows, width).transpose(1, 0, 2, 3)
        mixed_rows = exchange(mixed.reshape(n * slices, rows, width)).reshape(chans, count, width)

    d_mixed, d_gate, out_grads = call(
        "middle",
        functools.partial(middle_kernel, n if direct else 0),
        (layer_norm_gains, mixed_rows, d_outn, zn, cg, d_update, w_out),
        [smem, chan_spec, chan_spec, cat_spec, cat_spec, cat_spec, wo_spec],
        [chan_spec, cat_spec, full((n, 16, 2 * chans) if direct else (chans + 8, 2 * chans))],
        [
            jax.ShapeDtypeStruct((chans, count, width), BF16),
            cat(BF16),
            array((n, 16, 2 * chans), BF16) if direct else array((chans + 8, 2 * chans), F32),
        ],
        [scratch, pltpu.VMEM((chans, LANES), F32), pltpu.VMEM((chans, lanes), BF16)],
    )

    if direct:
        dmix_cols = exchange(d_mixed.reshape(n, per, count, width))
        d_lr = pl.pallas_call(
            functools.partial(triangle_back_kernel, rows),
            out_shape=jax.ShapeDtypeStruct((n, 2 * per + 1, count, width), BF16),
            compiler_params=params,
            name="triangle_back",
        )(dmix_cols, left_cols, right_cols, out_grads)
        d_lr = exchange(d_lr)
        d_lr_spec = whole
    else:
        dmix_cols = exchange(d_mixed.reshape(n * slices, rows, width)).reshape(n, slices, rows, width)
        dmix_cols = dmix_cols.transpose(1, 0, 2, 3).reshape(slices, width, width)
        d_left = jnp.einsum("sij,sjk->sik", dmix_cols, right_cols, preferred_element_type=F32)
        d_right = jnp.einsum("sij,sik->sjk", dmix_cols, left_cols, preferred_element_type=F32)
        d_lr = jnp.stack([d_left.astype(BF16), d_right.astype(BF16)]).reshape(2, slices, n, rows, width)
        d_lr = exchange(d_lr.transpose(2, 1, 0, 3, 4).reshape(n * slices, 2, rows, width))
        d_lr = d_lr.reshape(chans, templ, 2, rows, width).transpose(0, 2, 1, 3, 4)
        d_lr = d_lr.reshape(groups, 2 * per, count, width)
        d_lr_spec = lr_spec

    pair_grad, keep, send, done = call(
        "back",
        functools.partial(back_kernel, blocks),
        (me, d_lr, fac, zn, d_gate, normed, rstd, wcat, layer_norm_gains),
        [smem, d_lr_spec, fac_spec, cat_spec, cat_spec, cat_spec, one_spec, full((chans, 5 * chans)), gains_spec],
        [rows_spec, full((half_rows, 2 * chans)), full((half_rows, 2 * chans)), full((16, 2 * chans))],
        [
            jax.ShapeDtypeStruct((count, chans, width), BF16),
            array((half_rows, 2 * chans), F32),
            jax.ShapeDtypeStruct((half_rows, 2 * chans), F32),
            array((16, 2 * chans), F32),
        ],
        [scratch, scratch, pltpu.VMEM((5 * chans, lanes), BF16), pltpu.VMEM((2 * chans + 8, 2 * chans), F32)],
    )

    got = lax.ppermute(send, "row", [(d, d ^ 1) for d in range(n)])
    sums = pl.pallas_call(
        combine_kernel,
        out_shape=jax.ShapeDtypeStruct((n, chans + 16, 2 * chans), BF16),
        compiler_params=params,
        name="combine",
    )(keep, got, done)
    sums = exchange(sums)
    grad_proj, grad_out, norm_grads = pl.pallas_call(
        functools.partial(unpack_kernel, 1.0 / width, chans // n if direct else 0),
        out_shape=[
            jax.ShapeDtypeStruct(w_proj.shape, F32),
            jax.ShapeDtypeStruct(w_out.shape, F32),
            jax.ShapeDtypeStruct((3, chans), F32),
        ],
        compiler_params=params,
        name="unpack",
    )(sums, done if direct else lax.psum(out_grads, "row"))
    return pair_grad.reshape(pair.shape), grad_proj, grad_out, norm_grads


def solution(mesh):
    return jax.shard_map(
        functools.partial(per_device, mesh.shape["row"]),
        mesh=mesh,
        in_specs=(
            P("groups", "row", None, None),
            P("groups", "row", None, None),
            P("groups"),
            P("groups", None, None),
            P(),
            P(),
            P(),
            P(),
        ),
        out_specs=(
            P("groups", "row", None, None),
            P("groups", None, None),
            P("groups", None, None),
            P("groups", None),
        ),
        check_vma=False,
    )
```

```python
import functools

import jax
import jax.numpy as jnp
from jax import lax
from jax.experimental import pallas as pl
from jax.experimental.pallas import tpu as pltpu
from jax.sharding import PartitionSpec as P

EPS = 1e-05
LANES = 128
F32 = jnp.float32
BF16 = jnp.bfloat16


def dot(a, b):
    return jnp.dot(a, b, preferred_element_type=F32)


def dot_nt(a, b):
    return lax.dot_general(a, b, (((1,), (1,)), ((), ())), preferred_element_type=F32)


def dot_tn(a, b):
    return lax.dot_general(a, b, (((0,), (0,)), ((), ())), preferred_element_type=F32)


def transposed(weight):
    return weight.astype(F32).T.astype(BF16)


def column(row):
    n = row.shape[1]
    eye = lax.broadcasted_iota(jnp.int32, (n, n), 0) == lax.broadcasted_iota(jnp.int32, (n, n), 1)
    return jnp.sum(jnp.where(eye, row, 0.0), axis=1, keepdims=True)


def as_row(col):
    n = col.shape[0]
    eye = lax.broadcasted_iota(jnp.int32, (n, n), 0) == lax.broadcasted_iota(jnp.int32, (n, n), 1)
    return jnp.sum(jnp.where(eye, col, 0.0), axis=0, keepdims=True)


def layer_norm(x):
    mean = jnp.mean(x, axis=0, keepdims=True)
    centred = x - mean
    rstd = lax.rsqrt(jnp.mean(centred * centred, axis=0, keepdims=True) + EPS)
    return centred * rstd, rstd


def mask_rows(me_ref, tokens_ref, cover_ref, tok_ref, block, rows):
    width, (tiles, _, templ) = tokens_ref.shape[1], cover_ref.shape
    tile = width // tiles
    first = me_ref[0] * rows
    here = lax.broadcasted_iota(jnp.int32, (rows, width), 0) + first == lax.broadcasted_iota(jnp.int32, (rows, width), 1)
    row_mask = jnp.sum(jnp.where(here, tokens_ref[...].astype(F32), 0.0), axis=1, keepdims=True)
    column_mask = tok_ref[...].astype(F32)
    cover = cover_ref[first // tile].astype(F32)
    here = lax.broadcasted_iota(jnp.int32, (tiles, templ), 0) == block() * LANES // tile
    cover = jnp.sum(jnp.where(here, cover, 0.0), axis=0, keepdims=True)
    out = []
    for t in range(templ):
        masked = column_mask * cover[:, t:t + 1]
        out += [masked * row_mask[r:r + 1, :] for r in range(rows)]
    return out


def front_kernel(rows, block, me_ref, tokens_ref, cover_ref, pair_ref, cot_ref, tok_ref, w_ref, wo_ref, gains_ref, bias_ref, lr_ref, zn_ref, fac_ref, cg_ref, du_ref, normed_ref, rstd_ref, dout_ref, wcat_ref, left_scr, right_scr, dout_scr):
    count, chans, _ = pair_ref.shape
    wcat_ref[...] = jnp.concatenate([w_ref[0], w_ref[1], w_ref[2], w_ref[3], wo_ref[0]], axis=1)
    gain, bias = column(gains_ref[0:1, :]), column(bias_ref[...])
    masks = mask_rows(me_ref, tokens_ref, cover_ref, tok_ref, block, rows)
    weights = jnp.concatenate([transposed(w_ref[p]) for p in range(4)] + [transposed(wo_ref[0])], axis=0)
    w_back = wo_ref[1]
    for pos in range(0, count, 2):
        span = slice(pos * LANES, (pos + 2) * LANES)
        zn = []
        for q in (pos, pos + 1):
            normed, rstd = layer_norm(pair_ref[q].astype(F32))
            lanes = slice(q * LANES, (q + 1) * LANES)
            normed_ref[0, :, lanes] = normed
            rstd_ref[0, :, lanes] = rstd
            zn.append((normed * gain + bias).astype(BF16))
        zn = jnp.concatenate(zn, axis=1)
        zn_ref[0, :, span] = zn
        pre = dot(weights, zn)
        for j in range(2):
            part = pre[:, j * LANES:(j + 1) * LANES]
            pre_p = [part[p * chans:(p + 1) * chans] for p in range(5)]
            mask = masks[pos + j]
            where = pl.ds(pos + j, chans, stride=count)
            lanes = slice((pos + j) * LANES, (pos + j + 1) * LANES)
            for p, scr in ((0, left_scr), (2, right_scr)):
                sig = jax.nn.sigmoid(pre_p[p])
                sig_mask = sig * mask
                both = sig_mask * pre_p[p + 1]
                scr[where, :] = both
                fac_ref[0, p * chans:(p + 1) * chans, lanes] = both * (1.0 - sig)
                fac_ref[0, (p + 1) * chans:(p + 2) * chans, lanes] = sig_mask
            gate = jax.nn.sigmoid(pre_p[4])
            d_update = cot_ref[pos + j].astype(F32) * gate
            cg_ref[0, :, lanes] = d_update * (1.0 - gate)
            du_ref[0, :, lanes] = d_update.astype(BF16)
        d_outn = dot(w_back, du_ref[0, :, span])
        for j in range(2):
            dout_scr[pl.ds(pos + j, chans, stride=count), :] = d_outn[:, j * LANES:(j + 1) * LANES]
    groups, both, _, _ = lr_ref.shape
    per = both // 2
    lr_ref[:, 0:per] = left_scr[...].astype(BF16).reshape(groups, per, count, LANES)
    lr_ref[:, per:both] = right_scr[...].astype(BF16).reshape(groups, per, count, LANES)
    dout_ref[...] = dout_scr[...].reshape(chans, count, LANES)


def mixed_kernel(rows, cols_ref, mixed_ref, left_ref, right_ref):
    n, both, count, width = cols_ref.shape
    per, templ = both // 2, count // rows
    for c in range(per):
        left_all = cols_ref[:, c].astype(F32)
        right_all = cols_ref[:, per + c].astype(F32)
        parts = []
        for t in range(templ):
            left = left_all[:, t * rows:(t + 1) * rows].reshape(n * rows, width).astype(BF16)
            right = right_all[:, t * rows:(t + 1) * rows].reshape(n * rows, width).astype(BF16)
            left_ref[c * templ + t] = left
            right_ref[c * templ + t] = right
            parts.append(dot_nt(left, right).reshape(n, rows, width))
        mixed_ref[:, c] = jnp.concatenate(parts, axis=1).astype(BF16)


def triangle_back_kernel(rows, count, dmix_ref, left_ref, right_ref, out_ref, done_ref):
    n, length, width = dmix_ref.shape
    per, templ = length // count, count // rows
    for c in range(per):
        dmix_all = dmix_ref[:, c * count:(c + 1) * count].astype(F32)
        left_parts, right_parts = [], []
        for t in range(templ):
            dmix = dmix_all[:, t * rows:(t + 1) * rows].reshape(n * rows, width).astype(BF16)
            left_parts.append(dot(dmix, right_ref[c * templ + t]).reshape(n, rows, width))
            right_parts.append(dot_tn(dmix, left_ref[c * templ + t]).reshape(n, rows, width))
        out_ref[:, c] = jnp.concatenate(left_parts, axis=1).astype(BF16)
        out_ref[:, per + c] = jnp.concatenate(right_parts, axis=1).astype(BF16)
    done_ref[...] = jnp.sum(dmix_ref[:, per * count:].astype(F32), axis=0)


def split(x):
    high = x.astype(BF16).astype(F32)
    return high, x - high


def tree_sum(parts):
    while len(parts) > 1:
        parts = [a + b for a, b in zip(parts[::2], parts[1::2])] + parts[len(parts) // 2 * 2:]
    return parts[0]


def channel_sum(chans, value):
    accs = [None] * 4
    for c in range(chans):
        v = value(c)
        accs[c % 4] = v if accs[c % 4] is None else accs[c % 4] + v
    return tree_sum([a for a in accs if a is not None])


def middle_kernel(n, block, gains_ref, mixed_ref, dout_ref, zn_ref, cg_ref, du_ref, wo_ref, dmix_ref, dgate_ref, *rest_refs):
    *grads_refs, scr, norm_scr, outn_scr = rest_refs
    chans, count, _ = mixed_ref.shape
    inv = 1.0 / chans
    mean = channel_sum(chans, lambda c: mixed_ref[c].astype(F32)) * inv
    mean_h = channel_sum(chans, lambda c: dout_ref[c] * gains_ref[1, c]) * inv

    def squares(c):
        centred = mixed_ref[c].astype(F32) - mean
        return centred * centred

    rstd = lax.rsqrt(channel_sum(chans, squares) * inv + EPS)

    def products(c):
        gain = gains_ref[1, c]
        xhat = (mixed_ref[c].astype(F32) - mean) * rstd
        outn = xhat * gain
        scr[c * count:(c + 1) * count, :] = outn
        product = dout_ref[c] * xhat
        norm_scr[c:c + 1, :] = jnp.sum(product, axis=0, keepdims=True)
        return product * gain

    mean_p = channel_sum(chans, products) * inv
    for c in range(chans):
        xhat = (mixed_ref[c].astype(F32) - mean) * rstd
        d_mixed = (rstd * (dout_ref[c] * gains_ref[1, c] - mean_h - xhat * mean_p)).astype(BF16)
        if n:
            per = chans // n
            dmix_ref[c // per, c % per * count:(c % per + 1) * count] = d_mixed
        else:
            dmix_ref[c] = d_mixed
    w_update = transposed(wo_ref[1])
    for pos in range(count):
        span = slice(pos * LANES, (pos + 1) * LANES)
        outn_scr[:, span] = scr[pl.ds(pos, chans, stride=count), :].astype(BF16)
    update = dot(w_update, outn_scr[...])
    d_gate = (cg_ref[0] * update).astype(BF16)
    dgate_ref[0] = d_gate
    gate_grad = dot_nt(zn_ref[0], d_gate)
    out_grad = dot_nt(outn_scr[...], du_ref[0])
    norm = as_row(jnp.sum(norm_scr[...], axis=1, keepdims=True))
    if n:
        grads = jnp.concatenate([gate_grad, out_grad], axis=1)
        norm = jnp.concatenate([norm, jnp.zeros_like(norm)], axis=1)
        share = chans // n
        rest = jnp.zeros((6 - share, 2 * chans), F32)
        for d in range(n):
            tile = jnp.concatenate([grads[d * share:(d + 1) * share], *split(norm), rest], axis=0)
            dmix_ref[d, share * count:] = tile.astype(BF16)
        return
    grads_ref, = grads_refs

    @pl.when(block() == 0)
    def _():
        grads_ref[...] = jnp.zeros_like(grads_ref)

    grads_ref[0:chans, 0:chans] += gate_grad
    grads_ref[0:chans, chans:2 * chans] += out_grad
    grads_ref[chans:chans + 1, 0:chans] += norm


def back_kernel(blocks, block, me_ref, dlr_ref, fac_ref, zn_ref, dgate_ref, normed_ref, rstd_ref, wcat_ref, gains_ref, pair_ref, keep_ref, send_ref, left_scr, right_scr, d_scr, pack_scr):
    groups, parts, count, _ = dlr_ref.shape
    per = parts // 2
    chans = groups * per
    left_scr[...] = dlr_ref[:, 0:per].astype(F32).reshape(chans * count, LANES)
    right_scr[...] = dlr_ref[:, per:2 * per].astype(F32).reshape(chans * count, LANES)
    d_scr[4 * chans:5 * chans, :] = dgate_ref[0]
    for pos in range(count):
        span = slice(pos * LANES, (pos + 1) * LANES)
        where = pl.ds(pos, chans, stride=count)
        d_left, d_right = left_scr[where, :], right_scr[where, :]
        for p in range(4):
            d = d_left if p < 2 else d_right
            d_scr[p * chans:(p + 1) * chans, span] = (d * fac_ref[0, p * chans:(p + 1) * chans, span]).astype(BF16)
    d_zn = dot(wcat_ref[...], d_scr[...])
    gain = column(gains_ref[0:1, :])
    for pos in range(count):
        span = slice(pos * LANES, (pos + 1) * LANES)
        h = d_zn[:, span] * gain
        normed = normed_ref[0, :, span]
        mean_h = jnp.mean(h, axis=0, keepdims=True)
        mean_p = jnp.mean(h * normed, axis=0, keepdims=True)
        pair_ref[pos] = (rstd_ref[0, :, span] * (h - mean_h - normed * mean_p)).astype(BF16)
    grads = dot_nt(zn_ref[0], d_scr[0:4 * chans, :])
    bias_grad = as_row(jnp.sum(d_zn, axis=1, keepdims=True))
    gain_grad = as_row(jnp.sum(d_zn * normed_ref[0], axis=1, keepdims=True))

    @pl.when(block() == 0)
    def _():
        pack_scr[...] = jnp.zeros_like(pack_scr)

    pack_scr[0:chans, :] += grads[:, 0:2 * chans]
    pack_scr[chans:2 * chans, :] += grads[:, 2 * chans:4 * chans]
    pack_scr[2 * chans:2 * chans + 1, 0:chans] += gain_grad
    pack_scr[2 * chans + 1:2 * chans + 2, 0:chans] += bias_grad

    @pl.when(block() == blocks - 1)
    def _():
        half = me_ref[0] % 2
        own = pl.multiple_of(half * chans, 8)
        other = pl.multiple_of((1 - half) * chans, 8)
        keep_ref[0:chans, :] = pack_scr[pl.ds(own, chans), :]
        send_ref[0:chans, :] = pack_scr[pl.ds(other, chans), :]
        keep_ref[chans:chans + 8, :] = pack_scr[2 * chans:2 * chans + 8, :]
        send_ref[chans:chans + 8, :] = pack_scr[2 * chans:2 * chans + 8, :]


def combine_kernel(keep_ref, got_ref, done_ref, out_ref):
    rows = keep_ref.shape[0] - 8
    total = keep_ref[...] + got_ref[...]
    tile = jnp.concatenate([done_ref[0:4, :], *split(total[rows:rows + 2])], axis=0)
    block = jnp.concatenate([total[0:rows], tile], axis=0).astype(BF16)
    for d in range(out_ref.shape[0]):
        out_ref[d] = block


def total_kernel(pack_ref, mine_ref, norm_ref):
    chips, length, _ = pack_ref.shape
    rows = length - 8
    mine_ref[0:rows, :] = tree_sum([pack_ref[d, 0:rows, :].astype(F32) for d in range(chips)])
    tiles = [pack_ref[d, rows:, :].astype(F32) for d in range(chips)]
    for d in range(0, chips, 2):
        mine_ref[rows + 4 * d:rows + 4 * d + 8, :] = jnp.concatenate([tiles[d][0:4], tiles[d + 1][0:4]], axis=0)
    norm_ref[...] = tree_sum(tiles)


def unpack_kernel(scale, share, me_ref, mine_ref, got_ref, norm_ref, done_ref, proj_ref, out_ref, norms_ref):
    chans = proj_ref.shape[1]
    odd = me_ref[0] % 2 == 1
    mine, got = mine_ref[...] * scale, got_ref[...] * scale
    even_odd = (jnp.where(odd, got, mine), jnp.where(odd, mine, got))
    for half in range(2):
        proj_ref[2 * half] = even_odd[half][0:chans, 0:chans]
        proj_ref[2 * half + 1] = even_odd[half][0:chans, chans:2 * chans]
    norms_ref[0:2, :] = (norm_ref[4:6, 0:chans] + norm_ref[6:8, 0:chans]) * scale
    if share:
        norms_ref[2:3, :] = (done_ref[share:share + 1, 0:chans] + done_ref[share + 1:share + 2, 0:chans]) * scale
        for d in range(chans // share):
            start = chans + d // 2 * 4
            rows = even_odd[d % 2][start:start + share]
            for p in range(2):
                out_ref[p, d * share:(d + 1) * share] = rows[:, p * chans:(p + 1) * chans]
    else:
        norms_ref[2:3, :] = done_ref[chans:chans + 1, 0:chans] * scale
        for p in range(2):
            out_ref[p] = done_ref[0:chans, p * chans:(p + 1) * chans] * scale


def exchange(x, groups=None):
    return lax.all_to_all(x, "row", split_axis=0, concat_axis=0, axis_index_groups=groups, tiled=True)


def per_device(n, pair, cotangent, token_mask, coverage, w_proj, w_out, layer_norm_gains, ln_bias):
    templ, rows, chans, width = pair.shape
    count = templ * rows
    blocks = width // LANES
    direct = blocks == 1 and chans % n == 0 and chans // n <= 4
    groups = n if direct else chans
    per = chans // groups
    lanes = count * LANES
    me = lax.axis_index("row").astype(jnp.int32).reshape(1)
    tokens_row = token_mask.reshape(1, width)

    params = pltpu.CompilerParams(vmem_limit_bytes=(16 if blocks == 1 else 40) * 1024 * 1024)
    smem = pl.BlockSpec(memory_space=pltpu.SMEM)
    whole = pl.BlockSpec(memory_space=pltpu.VMEM)

    def block_spec(shape, index):
        return whole if blocks == 1 else pl.BlockSpec(shape, index)

    def full(shape):
        return block_spec(shape, lambda b: (0,) * len(shape))

    def array(shape, dtype):
        return pltpu.VMEM(shape, dtype) if blocks == 1 else jax.ShapeDtypeStruct(shape, dtype)

    def from_hbm(x):
        return pltpu.with_memory_space_constraint(x, pltpu.HBM)

    def call(name, kernel, args, in_specs, out_specs, out_shape, scratch_shapes=()):
        block = (lambda: 0) if blocks == 1 else (lambda: pl.program_id(0))
        kernel = functools.partial(kernel, block)
        return pl.pallas_call(
            kernel,
            grid=() if blocks == 1 else (blocks,),
            in_specs=in_specs,
            out_specs=out_specs,
            out_shape=out_shape,
            scratch_shapes=scratch_shapes,
            compiler_params=params,
            name=name,
        )(*args)

    rows_spec = block_spec((count, chans, LANES), lambda b: (0, 0, b))
    tok_spec = block_spec((1, LANES), lambda b: (0, b))
    lr_spec = block_spec((groups, 2 * per, count, LANES), lambda b: (0, 0, 0, b))
    cat_spec = block_spec((1, chans, lanes), lambda b: (b, 0, 0))
    fac_spec = block_spec((1, 4 * chans, lanes), lambda b: (b, 0, 0))
    one_spec = block_spec((1, 1, lanes), lambda b: (b, 0, 0))
    chan_spec = block_spec((chans, count, LANES), lambda b: (0, 0, b))
    w_spec, wo_spec, gains_spec = full(w_proj.shape), full(w_out.shape), full(layer_norm_gains.shape)
    scratch = pltpu.VMEM((chans * count, LANES), F32)
    pair_rows = from_hbm(pair.reshape(count, chans, width))
    cot_rows = from_hbm(cotangent.reshape(count, chans, width))
    w_proj_in, w_out_in, gains_in = from_hbm(w_proj), from_hbm(w_out), from_hbm(layer_norm_gains)
    tokens_in, cover_in = from_hbm(tokens_row), from_hbm(coverage.transpose(1, 2, 0))
    half_rows = chans + 8

    def cat(dtype):
        return array((blocks, chans, lanes), dtype)

    lr, zn, fac, cg, d_update, normed, rstd, d_outn, wcat = call(
        "front",
        functools.partial(front_kernel, rows),
        (me, tokens_in, cover_in, pair_rows, cot_rows, tokens_in, w_proj_in, w_out_in, gains_in, from_hbm(ln_bias.reshape(1, chans))),
        [smem, full((1, width)), full(cover_in.shape), rows_spec, rows_spec, tok_spec, w_spec, wo_spec, gains_spec, full((1, chans))],
        [lr_spec, cat_spec, fac_spec, cat_spec, cat_spec, cat_spec, one_spec, chan_spec, full((chans, 5 * chans))],
        [
            jax.ShapeDtypeStruct((groups, 2 * per, count, width), BF16),
            cat(BF16),
            array((blocks, 4 * chans, lanes), F32),
            cat(F32),
            cat(BF16),
            cat(F32),
            array((blocks, 1, lanes), F32),
            array((chans, count, width), F32),
            array((chans, 5 * chans), BF16),
        ],
        [scratch, scratch, scratch],
    )

    if direct:
        cols = exchange(lr)
        mixed, left_cols, right_cols = pl.pallas_call(
            functools.partial(mixed_kernel, rows),
            out_shape=[
                jax.ShapeDtypeStruct((n, per, count, width), BF16),
                array((per * templ, width, width), BF16),
                array((per * templ, width, width), BF16),
            ],
            compiler_params=params,
            name="mixed",
        )(cols)
        mixed_rows = exchange(mixed).reshape(chans, count, width)
    else:
        slices = chans * templ // n
        cols = lr.reshape(chans, 2, templ, rows, width).transpose(0, 2, 1, 3, 4)
        cols = exchange(cols.reshape(n * slices, 2, rows, width)).reshape(n, slices, 2, rows, width)
        left_cols, right_cols = cols.transpose(2, 1, 0, 3, 4).reshape(2, slices, width, width)
        mixed = jnp.einsum("sik,sjk->sij", left_cols, right_cols, preferred_element_type=F32)
        mixed = mixed.astype(BF16).reshape(slices, n, rows, width).transpose(1, 0, 2, 3)
        mixed_rows = exchange(mixed.reshape(n * slices, rows, width)).reshape(chans, count, width)

    dmix_shape = (n, per * count + 8, width) if direct else (chans, count, width)
    d_mixed, d_gate, *out_grads = call(
        "middle",
        functools.partial(middle_kernel, n if direct else 0),
        (layer_norm_gains, mixed_rows, d_outn, zn, cg, d_update, w_out),
        [smem, chan_spec, chan_spec, cat_spec, cat_spec, cat_spec, wo_spec],
        [full(dmix_shape) if direct else chan_spec, cat_spec] + [full((chans + 8, 2 * chans))] * (not direct),
        [jax.ShapeDtypeStruct(dmix_shape, BF16), cat(BF16)] + [array((chans + 8, 2 * chans), F32)] * (not direct),
        [scratch, pltpu.VMEM((chans, LANES), F32), pltpu.VMEM((chans, lanes), BF16)],
    )

    if direct:
        d_lr, done = pl.pallas_call(
            functools.partial(triangle_back_kernel, rows, count),
            out_shape=[jax.ShapeDtypeStruct((n, 2 * per, count, width), BF16), array((8, width), F32)],
            compiler_params=params,
            name="triangle_back",
        )(exchange(d_mixed), left_cols, right_cols)
        d_lr = exchange(d_lr)
    else:
        dmix_cols = exchange(d_mixed.reshape(n * slices, rows, width)).reshape(n, slices, rows, width)
        dmix_cols = dmix_cols.transpose(1, 0, 2, 3).reshape(slices, width, width)
        d_left = jnp.einsum("sij,sjk->sik", dmix_cols, right_cols, preferred_element_type=F32)
        d_right = jnp.einsum("sij,sik->sjk", dmix_cols, left_cols, preferred_element_type=F32)
        d_lr = jnp.stack([d_left.astype(BF16), d_right.astype(BF16)]).reshape(2, slices, n, rows, width)
        d_lr = exchange(d_lr.transpose(2, 1, 0, 3, 4).reshape(n * slices, 2, rows, width))
        d_lr = d_lr.reshape(chans, templ, 2, rows, width).transpose(0, 2, 1, 3, 4)
        d_lr = d_lr.reshape(groups, 2 * per, count, width)
        done = jnp.zeros((8, 2 * chans), F32)

    pair_grad, keep, send = call(
        "back",
        functools.partial(back_kernel, blocks),
        (me, d_lr, fac, zn, d_gate, normed, rstd, wcat, layer_norm_gains),
        [smem, lr_spec, fac_spec, cat_spec, cat_spec, cat_spec, one_spec, full((chans, 5 * chans)), gains_spec],
        [rows_spec, full((half_rows, 2 * chans)), full((half_rows, 2 * chans))],
        [
            jax.ShapeDtypeStruct((count, chans, width), BF16),
            array((half_rows, 2 * chans), F32),
            jax.ShapeDtypeStruct((half_rows, 2 * chans), F32),
        ],
        [scratch, scratch, pltpu.VMEM((5 * chans, lanes), BF16), pltpu.VMEM((2 * chans + 8, 2 * chans), F32)],
    )

    partner = [(d, d ^ 1) for d in range(n)]
    got = lax.ppermute(send, "row", partner)
    sums = pl.pallas_call(
        combine_kernel,
        out_shape=jax.ShapeDtypeStruct((n // 2, half_rows, 2 * chans), BF16),
        compiler_params=params,
        name="combine",
    )(keep, got, done)
    sums = exchange(sums, [list(range(core, n, 2)) for core in range(2)])
    mine, norms = pl.pallas_call(
        total_kernel,
        out_shape=[jax.ShapeDtypeStruct((chans + 2 * n, 2 * chans), F32), jax.ShapeDtypeStruct((8, 2 * chans), F32)],
        compiler_params=params,
        name="total",
    )(sums)
    got = lax.ppermute(mine, "row", partner)
    grad_proj, grad_out, norm_grads = pl.pallas_call(
        functools.partial(unpack_kernel, 1.0 / width, chans // n if direct else 0),
        in_specs=[smem] + [whole] * 4,
        out_shape=[
            jax.ShapeDtypeStruct(w_proj.shape, F32),
            jax.ShapeDtypeStruct(w_out.shape, F32),
            jax.ShapeDtypeStruct((3, chans), F32),
        ],
        compiler_params=params,
        name="unpack",
    )(me, mine, got, norms, done if direct else lax.psum(out_grads[0], "row"))
    return pair_grad.reshape(pair.shape), grad_proj, grad_out, norm_grads


def solution(mesh):
    return jax.shard_map(
        functools.partial(per_device, mesh.shape["row"]),
        mesh=mesh,
        in_specs=(
            P("groups", "row", None, None),
            P("groups", "row", None, None),
            P("groups"),
            P("groups", None, None),
            P(),
            P(),
            P(),
            P(),
        ),
        out_specs=(
            P("groups", "row", None, None),
            P("groups", None, None),
            P("groups", None, None),
            P("groups", None),
        ),
        check_vma=False,
    )
```

```python
import functools

import jax
import jax.numpy as jnp
from jax import lax
from jax.experimental import pallas as pl
from jax.experimental.pallas import tpu as pltpu
from jax.sharding import PartitionSpec as P

EPS = 1e-05
LANES = 128
F32 = jnp.float32
BF16 = jnp.bfloat16


def dot(a, b):
    return jnp.dot(a, b, preferred_element_type=F32)


def dot_nt(a, b):
    return lax.dot_general(a, b, (((1,), (1,)), ((), ())), preferred_element_type=F32)


def dot_tn(a, b):
    return lax.dot_general(a, b, (((0,), (0,)), ((), ())), preferred_element_type=F32)


def transposed(weight):
    return weight.astype(F32).T.astype(BF16)


def column(row):
    n = row.shape[1]
    eye = lax.broadcasted_iota(jnp.int32, (n, n), 0) == lax.broadcasted_iota(jnp.int32, (n, n), 1)
    return jnp.sum(jnp.where(eye, row, 0.0), axis=1, keepdims=True)


def as_row(col):
    n = col.shape[0]
    eye = lax.broadcasted_iota(jnp.int32, (n, n), 0) == lax.broadcasted_iota(jnp.int32, (n, n), 1)
    return jnp.sum(jnp.where(eye, col, 0.0), axis=0, keepdims=True)


def layer_norm(x):
    mean = jnp.mean(x, axis=0, keepdims=True)
    centred = x - mean
    rstd = lax.rsqrt(jnp.mean(centred * centred, axis=0, keepdims=True) + EPS)
    return centred * rstd, rstd


def mask_rows(me_ref, tokens_ref, cover_ref, tok_ref, block, rows):
    width, (tiles, _, templ) = tokens_ref.shape[1], cover_ref.shape
    tile = width // tiles
    first = me_ref[0] * rows
    here = lax.broadcasted_iota(jnp.int32, (rows, width), 0) + first == lax.broadcasted_iota(jnp.int32, (rows, width), 1)
    row_mask = jnp.sum(jnp.where(here, tokens_ref[...].astype(F32), 0.0), axis=1, keepdims=True)
    column_mask = tok_ref[...].astype(F32)
    cover = cover_ref[first // tile].astype(F32)
    here = lax.broadcasted_iota(jnp.int32, (tiles, templ), 0) == block() * LANES // tile
    cover = jnp.sum(jnp.where(here, cover, 0.0), axis=0, keepdims=True)
    out = []
    for t in range(templ):
        masked = column_mask * cover[:, t:t + 1]
        out += [masked * row_mask[r:r + 1, :] for r in range(rows)]
    return out


def front_kernel(rows, block, me_ref, tokens_ref, cover_ref, pair_ref, cot_ref, tok_ref, w_ref, wo_ref, gains_ref, bias_ref, lr_ref, zn_ref, fac_ref, cg_ref, du_ref, normed_ref, rstd_ref, dout_ref, wcat_ref, left_scr, right_scr, dout_scr):
    count, chans, _ = pair_ref.shape
    wcat_ref[...] = jnp.concatenate([w_ref[0], w_ref[1], w_ref[2], w_ref[3], wo_ref[0]], axis=1)
    gain, bias = column(gains_ref[0:1, :]), column(bias_ref[...])
    masks = mask_rows(me_ref, tokens_ref, cover_ref, tok_ref, block, rows)
    weights = jnp.concatenate([transposed(w_ref[p]) for p in range(4)] + [transposed(wo_ref[0])], axis=0)
    w_back = wo_ref[1]
    for q in range(count):
        normed, rstd = layer_norm(pair_ref[q].astype(F32))
        lanes = slice(q * LANES, (q + 1) * LANES)
        normed_ref[0, :, lanes] = normed
        rstd_ref[0, :, lanes] = rstd
        zn_ref[0, :, lanes] = (normed * gain + bias).astype(BF16)
    for pos in range(0, count, 8):
        pre = dot(weights, zn_ref[0, :, pos * LANES:(pos + 8) * LANES])
        for j in range(8):
            part = pre[:, j * LANES:(j + 1) * LANES]
            pre_p = [part[p * chans:(p + 1) * chans] for p in range(5)]
            mask = masks[pos + j]
            where = pl.ds(pos + j, chans, stride=count)
            lanes = slice((pos + j) * LANES, (pos + j + 1) * LANES)
            for p, scr in ((0, left_scr), (2, right_scr)):
                sig = jax.nn.sigmoid(pre_p[p])
                sig_mask = sig * mask
                both = sig_mask * pre_p[p + 1]
                scr[where, :] = both
                fac_ref[0, p * chans:(p + 1) * chans, lanes] = both * (1.0 - sig)
                fac_ref[0, (p + 1) * chans:(p + 2) * chans, lanes] = sig_mask
            gate = jax.nn.sigmoid(pre_p[4])
            d_update = cot_ref[pos + j].astype(F32) * gate
            cg_ref[0, :, lanes] = d_update * (1.0 - gate)
            du_ref[0, :, lanes] = d_update.astype(BF16)
    d_outn = dot(w_back, du_ref[0])
    for pos in range(count):
        dout_scr[pl.ds(pos, chans, stride=count), :] = d_outn[:, pos * LANES:(pos + 1) * LANES]
    groups, both, _, _ = lr_ref.shape
    per = both // 2
    lr_ref[:, 0:per] = left_scr[...].astype(BF16).reshape(groups, per, count, LANES)
    lr_ref[:, per:both] = right_scr[...].astype(BF16).reshape(groups, per, count, LANES)
    dout_ref[...] = dout_scr[...].reshape(chans, count, LANES)


def mixed_kernel(rows, cols_ref, mixed_ref, left_ref, right_ref):
    n, both, count, width = cols_ref.shape
    per, templ = both // 2, count // rows
    for c in range(per):
        left_all = cols_ref[:, c].astype(F32)
        right_all = cols_ref[:, per + c].astype(F32)
        parts = []
        for t in range(templ):
            left = left_all[:, t * rows:(t + 1) * rows].reshape(n * rows, width).astype(BF16)
            right = right_all[:, t * rows:(t + 1) * rows].reshape(n * rows, width).astype(BF16)
            left_ref[c * templ + t] = left
            right_ref[c * templ + t] = right
            parts.append(dot_nt(left, right).reshape(n, rows, width))
        mixed_ref[:, c] = jnp.concatenate(parts, axis=1).astype(BF16)


def triangle_back_kernel(rows, count, dmix_ref, left_ref, right_ref, out_ref, done_ref):
    n, length, width = dmix_ref.shape
    per, templ = length // count, count // rows
    for c in range(per):
        dmix_all = dmix_ref[:, c * count:(c + 1) * count].astype(F32)
        left_parts, right_parts = [], []
        for t in range(templ):
            dmix = dmix_all[:, t * rows:(t + 1) * rows].reshape(n * rows, width).astype(BF16)
            left_parts.append(dot(dmix, right_ref[c * templ + t]).reshape(n, rows, width))
            right_parts.append(dot_tn(dmix, left_ref[c * templ + t]).reshape(n, rows, width))
        out_ref[:, c] = jnp.concatenate(left_parts, axis=1).astype(BF16)
        out_ref[:, per + c] = jnp.concatenate(right_parts, axis=1).astype(BF16)
    done_ref[...] = jnp.sum(dmix_ref[:, per * count:].astype(F32), axis=0)


def split(x):
    high = x.astype(BF16).astype(F32)
    return high, x - high


def tree_sum(parts):
    while len(parts) > 1:
        parts = [a + b for a, b in zip(parts[::2], parts[1::2])] + parts[len(parts) // 2 * 2:]
    return parts[0]


def channel_sums(chans, values, scale):
    accs = [None] * 4
    for c in range(chans):
        v = values(c)
        accs[c % 4] = v if accs[c % 4] is None else [a + b for a, b in zip(accs[c % 4], v)]
    return [tree_sum(list(parts)) * scale for parts in zip(*accs)]


def middle_kernel(n, block, gains_ref, mixed_ref, dout_ref, zn_ref, cg_ref, du_ref, wo_ref, dmix_ref, dgate_ref, *rest_refs):
    *grads_refs, scr, norm_scr, outn_scr = rest_refs
    chans, count, _ = mixed_ref.shape
    inv = 1.0 / chans
    mean, mean_h = channel_sums(chans, lambda c: (mixed_ref[c].astype(F32), dout_ref[c] * gains_ref[1, c]), inv)

    def moments(c):
        centred = mixed_ref[c].astype(F32) - mean
        return centred * centred, dout_ref[c] * gains_ref[1, c] * centred

    variance, mean_p = channel_sums(chans, moments, inv)
    rstd = lax.rsqrt(variance + EPS)
    mean_p = mean_p * rstd
    per = chans // n if n else 1
    for c in range(chans):
        gain = gains_ref[1, c]
        xhat = (mixed_ref[c].astype(F32) - mean) * rstd
        scr[c * count:(c + 1) * count, :] = xhat * gain
        norm_scr[c:c + 1, :] = jnp.sum(dout_ref[c] * xhat, axis=0, keepdims=True)
        d_mixed = (rstd * (dout_ref[c] * gain - mean_h - xhat * mean_p)).astype(BF16)
        if n:
            dmix_ref[c // per, c % per * count:(c % per + 1) * count] = d_mixed
        else:
            dmix_ref[c] = d_mixed
    w_update = transposed(wo_ref[1])
    for pos in range(count):
        span = slice(pos * LANES, (pos + 1) * LANES)
        outn_scr[:, span] = scr[pl.ds(pos, chans, stride=count), :].astype(BF16)
    update = dot(w_update, outn_scr[...])
    d_gate = (cg_ref[0] * update).astype(BF16)
    dgate_ref[0] = d_gate
    gate_grad = dot_nt(zn_ref[0], d_gate)
    out_grad = dot_nt(outn_scr[...], du_ref[0])
    norm = as_row(jnp.sum(norm_scr[...], axis=1, keepdims=True))
    if n:
        grads = jnp.concatenate([gate_grad, out_grad], axis=1)
        norm = jnp.concatenate([norm, jnp.zeros_like(norm)], axis=1)
        share = chans // n
        scr[0:chans, :] = grads
        tiles = pl.ds(chans, 8 * n)
        scr[tiles, :] = jnp.zeros((8 * n, 2 * chans), F32)
        for r in range(share):
            scr[pl.ds(chans + r, n, stride=8), :] = scr[pl.ds(r, n, stride=share), :]
        for r, row in enumerate(split(norm)):
            scr[pl.ds(chans + share + r, n, stride=8), :] = jnp.broadcast_to(row, (n, 2 * chans))
        dmix_ref[:, share * count:] = scr[tiles, :].reshape(n, 8, 2 * chans).astype(BF16)
        return
    grads_ref, = grads_refs

    @pl.when(block() == 0)
    def _():
        grads_ref[...] = jnp.zeros_like(grads_ref)

    grads_ref[0:chans, 0:chans] += gate_grad
    grads_ref[0:chans, chans:2 * chans] += out_grad
    grads_ref[chans:chans + 1, 0:chans] += norm


def gating_back_kernel(blocks, block, me_ref, dlr_ref, fac_ref, zn_ref, d_ref, keep_ref, send_ref, left_scr, right_scr, pack_scr):
    groups, parts, count, _ = dlr_ref.shape
    per = parts // 2
    chans = groups * per
    left_scr[...] = dlr_ref[:, 0:per].astype(F32).reshape(chans * count, LANES)
    right_scr[...] = dlr_ref[:, per:parts].astype(F32).reshape(chans * count, LANES)
    for pos in range(count):
        span = slice(pos * LANES, (pos + 1) * LANES)
        where = pl.ds(pos, chans, stride=count)
        d_left, d_right = left_scr[where, :], right_scr[where, :]
        for p in range(4):
            d = d_left if p < 2 else d_right
            d_ref[0, p * chans:(p + 1) * chans, span] = (d * fac_ref[0, p * chans:(p + 1) * chans, span]).astype(BF16)
    grads = dot_nt(zn_ref[0], d_ref[0])

    @pl.when(block() == 0)
    def _():
        pack_scr[...] = jnp.zeros_like(pack_scr)

    pack_scr[0:chans, :] += grads[:, 0:2 * chans]
    pack_scr[chans:2 * chans, :] += grads[:, 2 * chans:4 * chans]

    @pl.when(block() == blocks - 1)
    def _():
        half = me_ref[0] % 2
        keep_ref[...] = pack_scr[pl.ds(pl.multiple_of(half * chans, 8), chans), :]
        send_ref[...] = pack_scr[pl.ds(pl.multiple_of((1 - half) * chans, 8), chans), :]


def pair_grad_kernel(block, d_ref, dgate_ref, normed_ref, rstd_ref, wcat_ref, gains_ref, pair_ref, norm_ref):
    chans, count = normed_ref.shape[1], normed_ref.shape[2] // LANES
    d_zn = dot(wcat_ref[:, 0:4 * chans], d_ref[0]) + dot(wcat_ref[:, 4 * chans:5 * chans], dgate_ref[0])
    gain = column(gains_ref[0:1, :])
    for pos in range(count):
        span = slice(pos * LANES, (pos + 1) * LANES)
        h = d_zn[:, span] * gain
        normed = normed_ref[0, :, span]
        mean_h = jnp.mean(h, axis=0, keepdims=True)
        mean_p = jnp.mean(h * normed, axis=0, keepdims=True)
        pair_ref[pos] = (rstd_ref[0, :, span] * (h - mean_h - normed * mean_p)).astype(BF16)

    @pl.when(block() == 0)
    def _():
        norm_ref[...] = jnp.zeros_like(norm_ref)

    norm_ref[0:1, 0:chans] += as_row(jnp.sum(d_zn * normed_ref[0], axis=1, keepdims=True))
    norm_ref[1:2, 0:chans] += as_row(jnp.sum(d_zn, axis=1, keepdims=True))


def combine_kernel(keep_ref, got_ref, done_ref, norm_ref, out_ref):
    tile = jnp.concatenate([done_ref[0:4, :], *split(norm_ref[0:2, :])], axis=0)
    block = jnp.concatenate([keep_ref[...] + got_ref[...], tile], axis=0).astype(BF16)
    for d in range(out_ref.shape[0]):
        out_ref[d] = block


def total_kernel(pack_ref, mine_ref):
    chips, length, _ = pack_ref.shape
    rows = length - 8
    mine_ref[0:rows, :] = tree_sum([pack_ref[d, 0:rows, :].astype(F32) for d in range(chips)])
    tiles = [pack_ref[d, rows:, :].astype(F32) for d in range(chips)]
    for d in range(0, chips, 2):
        mine_ref[rows + 4 * d:rows + 4 * d + 8, :] = jnp.concatenate([tiles[d][0:4], tiles[d + 1][0:4]], axis=0)
    mine_ref[rows + 4 * chips:, :] = tree_sum(tiles)


def unpack_kernel(scale, share, me_ref, mine_ref, got_ref, done_ref, proj_ref, out_ref, norms_ref):
    chans = proj_ref.shape[1]
    odd = me_ref[0] % 2 == 1
    mine, got = mine_ref[...] * scale, got_ref[...] * scale
    even_odd = (jnp.where(odd, got, mine), jnp.where(odd, mine, got))
    for half in range(2):
        proj_ref[2 * half] = even_odd[half][0:chans, 0:chans]
        proj_ref[2 * half + 1] = even_odd[half][0:chans, chans:2 * chans]
    norm = (mine + got)[mine.shape[0] - 4:, 0:chans]
    norms_ref[0:2, :] = norm[0:2] + norm[2:4]
    if share:
        norms_ref[2:3, :] = (done_ref[share:share + 1, 0:chans] + done_ref[share + 1:share + 2, 0:chans]) * scale
        for d in range(chans // share):
            start = chans + d // 2 * 4
            rows = even_odd[d % 2][start:start + share]
            for p in range(2):
                out_ref[p, d * share:(d + 1) * share] = rows[:, p * chans:(p + 1) * chans]
    else:
        norms_ref[2:3, :] = done_ref[chans:chans + 1, 0:chans] * scale
        for p in range(2):
            out_ref[p] = done_ref[0:chans, p * chans:(p + 1) * chans] * scale


def exchange(x, groups=None):
    return lax.all_to_all(x, "row", split_axis=0, concat_axis=0, axis_index_groups=groups, tiled=True)


def per_device(n, pair, cotangent, token_mask, coverage, w_proj, w_out, layer_norm_gains, ln_bias):
    templ, rows, chans, width = pair.shape
    count = templ * rows
    blocks = width // LANES
    direct = blocks == 1 and chans % n == 0 and chans // n <= 4
    groups = n if direct else chans
    per = chans // groups
    lanes = count * LANES
    me = lax.axis_index("row").astype(jnp.int32).reshape(1)
    tokens_row = token_mask.reshape(1, width)

    params = pltpu.CompilerParams(vmem_limit_bytes=(16 if blocks == 1 else 40) * 1024 * 1024)
    smem = pl.BlockSpec(memory_space=pltpu.SMEM)
    whole = pl.BlockSpec(memory_space=pltpu.VMEM)

    def block_spec(shape, index):
        return whole if blocks == 1 else pl.BlockSpec(shape, index)

    def full(shape):
        return block_spec(shape, lambda b: (0,) * len(shape))

    def array(shape, dtype):
        return pltpu.VMEM(shape, dtype) if blocks == 1 else jax.ShapeDtypeStruct(shape, dtype)

    def from_hbm(x):
        return pltpu.with_memory_space_constraint(x, pltpu.HBM)

    def call(name, kernel, args, in_specs, out_specs, out_shape, scratch_shapes=()):
        block = (lambda: 0) if blocks == 1 else (lambda: pl.program_id(0))
        kernel = functools.partial(kernel, block)
        return pl.pallas_call(
            kernel,
            grid=() if blocks == 1 else (blocks,),
            in_specs=in_specs,
            out_specs=out_specs,
            out_shape=out_shape,
            scratch_shapes=scratch_shapes,
            compiler_params=params,
            name=name,
        )(*args)

    rows_spec = block_spec((count, chans, LANES), lambda b: (0, 0, b))
    tok_spec = block_spec((1, LANES), lambda b: (0, b))
    lr_spec = block_spec((groups, 2 * per, count, LANES), lambda b: (0, 0, 0, b))
    cat_spec = block_spec((1, chans, lanes), lambda b: (b, 0, 0))
    fac_spec = block_spec((1, 4 * chans, lanes), lambda b: (b, 0, 0))
    one_spec = block_spec((1, 1, lanes), lambda b: (b, 0, 0))
    chan_spec = block_spec((chans, count, LANES), lambda b: (0, 0, b))
    w_spec, wo_spec, gains_spec = full(w_proj.shape), full(w_out.shape), full(layer_norm_gains.shape)
    scratch = pltpu.VMEM((chans * count, LANES), F32)
    pair_rows = from_hbm(pair.reshape(count, chans, width))
    cot_rows = from_hbm(cotangent.reshape(count, chans, width))
    w_proj_in, w_out_in, gains_in = from_hbm(w_proj), from_hbm(w_out), from_hbm(layer_norm_gains)
    tokens_in, cover_in = from_hbm(tokens_row), from_hbm(coverage.transpose(1, 2, 0))

    def cat(dtype):
        return array((blocks, chans, lanes), dtype)

    lr, zn, fac, cg, d_update, normed, rstd, d_outn, wcat = call(
        "front",
        functools.partial(front_kernel, rows),
        (me, tokens_in, cover_in, pair_rows, cot_rows, tokens_in, w_proj_in, w_out_in, gains_in, from_hbm(ln_bias.reshape(1, chans))),
        [smem, full((1, width)), full(cover_in.shape), rows_spec, rows_spec, tok_spec, w_spec, wo_spec, gains_spec, full((1, chans))],
        [lr_spec, cat_spec, fac_spec, cat_spec, cat_spec, cat_spec, one_spec, chan_spec, full((chans, 5 * chans))],
        [
            jax.ShapeDtypeStruct((groups, 2 * per, count, width), BF16),
            cat(BF16),
            array((blocks, 4 * chans, lanes), F32),
            cat(F32),
            cat(BF16),
            cat(F32),
            array((blocks, 1, lanes), F32),
            array((chans, count, width), F32),
            array((chans, 5 * chans), BF16),
        ],
        [scratch, scratch, scratch],
    )

    if direct:
        cols = exchange(lr)
        mixed, left_cols, right_cols = pl.pallas_call(
            functools.partial(mixed_kernel, rows),
            out_shape=[
                jax.ShapeDtypeStruct((n, per, count, width), BF16),
                array((per * templ, width, width), BF16),
                array((per * templ, width, width), BF16),
            ],
            compiler_params=params,
            name="mixed",
        )(cols)
        mixed_rows = exchange(mixed).reshape(chans, count, width)
    else:
        slices = chans * templ // n
        cols = lr.reshape(chans, 2, templ, rows, width).transpose(0, 2, 1, 3, 4)
        cols = exchange(cols.reshape(n * slices, 2, rows, width)).reshape(n, slices, 2, rows, width)
        left_cols, right_cols = cols.transpose(2, 1, 0, 3, 4).reshape(2, slices, width, width)
        mixed = jnp.einsum("sik,sjk->sij", left_cols, right_cols, preferred_element_type=F32)
        mixed = mixed.astype(BF16).reshape(slices, n, rows, width).transpose(1, 0, 2, 3)
        mixed_rows = exchange(mixed.reshape(n * slices, rows, width)).reshape(chans, count, width)

    dmix_shape = (n, per * count + 8, width) if direct else (chans, count, width)
    d_mixed, d_gate, *out_grads = call(
        "middle",
        functools.partial(middle_kernel, n if direct else 0),
        (layer_norm_gains, mixed_rows, d_outn, zn, cg, d_update, w_out),
        [smem, chan_spec, chan_spec, cat_spec, cat_spec, cat_spec, wo_spec],
        [full(dmix_shape) if direct else chan_spec, cat_spec] + [full((chans + 8, 2 * chans))] * (not direct),
        [jax.ShapeDtypeStruct(dmix_shape, BF16), cat(BF16)] + [array((chans + 8, 2 * chans), F32)] * (not direct),
        [scratch, pltpu.VMEM((chans, LANES), F32), pltpu.VMEM((chans, lanes), BF16)],
    )

    if direct:
        d_lr, done = pl.pallas_call(
            functools.partial(triangle_back_kernel, rows, count),
            out_shape=[jax.ShapeDtypeStruct((n, 2 * per, count, width), BF16), array((8, width), F32)],
            compiler_params=params,
            name="triangle_back",
        )(exchange(d_mixed), left_cols, right_cols)
        d_lr = exchange(d_lr)
    else:
        dmix_cols = exchange(d_mixed.reshape(n * slices, rows, width)).reshape(n, slices, rows, width)
        dmix_cols = dmix_cols.transpose(1, 0, 2, 3).reshape(slices, width, width)
        d_left = jnp.einsum("sij,sjk->sik", dmix_cols, right_cols, preferred_element_type=F32)
        d_right = jnp.einsum("sij,sik->sjk", dmix_cols, left_cols, preferred_element_type=F32)
        d_lr = jnp.stack([d_left.astype(BF16), d_right.astype(BF16)]).reshape(2, slices, n, rows, width)
        d_lr = exchange(d_lr.transpose(2, 1, 0, 3, 4).reshape(n * slices, 2, rows, width))
        d_lr = d_lr.reshape(chans, templ, 2, rows, width).transpose(0, 2, 1, 3, 4)
        d_lr = d_lr.reshape(groups, 2 * per, count, width)
        done = jnp.zeros((8, 2 * chans), F32)

    d_spec = block_spec((1, 4 * chans, lanes), lambda b: (b, 0, 0))
    d_pre, keep, send = call(
        "gating_back",
        functools.partial(gating_back_kernel, blocks),
        (me, d_lr, fac, zn),
        [smem, lr_spec, fac_spec, cat_spec],
        [d_spec, full((chans, 2 * chans)), full((chans, 2 * chans))],
        [
            array((blocks, 4 * chans, lanes), BF16),
            array((chans, 2 * chans), F32),
            jax.ShapeDtypeStruct((chans, 2 * chans), F32),
        ],
        [scratch, scratch, pltpu.VMEM((2 * chans, 2 * chans), F32)],
    )

    pair_grad, norm_rows = call(
        "pair_grad",
        pair_grad_kernel,
        (d_pre, d_gate, normed, rstd, wcat, layer_norm_gains),
        [d_spec, cat_spec, cat_spec, one_spec, full((chans, 5 * chans)), gains_spec],
        [rows_spec, full((8, 2 * chans))],
        [jax.ShapeDtypeStruct((count, chans, width), BF16), array((8, 2 * chans), F32)],
    )

    partner = [(d, d ^ 1) for d in range(n)]
    got = lax.ppermute(send, "row", partner)
    sums = pl.pallas_call(
        combine_kernel,
        out_shape=jax.ShapeDtypeStruct((n // 2, chans + 8, 2 * chans), BF16),
        compiler_params=params,
        name="combine",
    )(keep, got, done, norm_rows)
    sums = exchange(sums, [list(range(core, n, 2)) for core in range(2)])
    mine = pl.pallas_call(
        total_kernel,
        out_shape=jax.ShapeDtypeStruct((chans + 2 * n + 8, 2 * chans), F32),
        compiler_params=params,
        name="total",
    )(sums)
    got = lax.ppermute(mine, "row", partner)
    grad_proj, grad_out, norm_grads = pl.pallas_call(
        functools.partial(unpack_kernel, 1.0 / width, chans // n if direct else 0),
        in_specs=[smem] + [whole] * 3,
        out_shape=[
            jax.ShapeDtypeStruct(w_proj.shape, F32),
            jax.ShapeDtypeStruct(w_out.shape, F32),
            jax.ShapeDtypeStruct((3, chans), F32),
        ],
        compiler_params=params,
        name="unpack",
    )(me, mine, got, done if direct else lax.psum(out_grads[0], "row"))
    return pair_grad.reshape(pair.shape), grad_proj, grad_out, norm_grads


def solution(mesh):
    return jax.shard_map(
        functools.partial(per_device, mesh.shape["row"]),
        mesh=mesh,
        in_specs=(
            P("groups", "row", None, None),
            P("groups", "row", None, None),
            P("groups"),
            P("groups", None, None),
            P(),
            P(),
            P(),
            P(),
        ),
        out_specs=(
            P("groups", "row", None, None),
            P("groups", None, None),
            P("groups", None, None),
            P("groups", None),
        ),
        check_vma=False,
    )
```

```python
import functools

import jax
import jax.numpy as jnp
from jax import lax
from jax.experimental import pallas as pl
from jax.experimental.pallas import tpu as pltpu
from jax.sharding import PartitionSpec as P

EPS = 1e-05
LANES = 128
F32 = jnp.float32
BF16 = jnp.bfloat16


def dot(a, b):
    return jnp.dot(a, b, preferred_element_type=F32)


def dot_nt(a, b):
    return lax.dot_general(a, b, (((1,), (1,)), ((), ())), preferred_element_type=F32)


def dot_tn(a, b):
    return lax.dot_general(a, b, (((0,), (0,)), ((), ())), preferred_element_type=F32)


def transposed(weight):
    return weight.astype(F32).T.astype(BF16)


def column(row):
    n = row.shape[1]
    eye = lax.broadcasted_iota(jnp.int32, (n, n), 0) == lax.broadcasted_iota(jnp.int32, (n, n), 1)
    return jnp.sum(jnp.where(eye, row, 0.0), axis=1, keepdims=True)


def as_row(col):
    n = col.shape[0]
    eye = lax.broadcasted_iota(jnp.int32, (n, n), 0) == lax.broadcasted_iota(jnp.int32, (n, n), 1)
    return jnp.sum(jnp.where(eye, col, 0.0), axis=0, keepdims=True)


def layer_norm(x):
    mean = jnp.mean(x, axis=0, keepdims=True)
    centred = x - mean
    rstd = lax.rsqrt(jnp.mean(centred * centred, axis=0, keepdims=True) + EPS)
    return centred * rstd, rstd


def mask_rows(me_ref, tokens_ref, cover_ref, tok_ref, block, rows):
    width, (tiles, _, templ) = tokens_ref.shape[1], cover_ref.shape
    tile = width // tiles
    first = me_ref[0] * rows
    here = lax.broadcasted_iota(jnp.int32, (rows, width), 0) + first == lax.broadcasted_iota(jnp.int32, (rows, width), 1)
    row_mask = jnp.sum(jnp.where(here, tokens_ref[...].astype(F32), 0.0), axis=1, keepdims=True)
    column_mask = tok_ref[...].astype(F32)
    cover = cover_ref[first // tile].astype(F32)
    here = lax.broadcasted_iota(jnp.int32, (tiles, templ), 0) == block() * LANES // tile
    cover = jnp.sum(jnp.where(here, cover, 0.0), axis=0, keepdims=True)
    out = []
    for t in range(templ):
        masked = column_mask * cover[:, t:t + 1]
        out += [masked * row_mask[r:r + 1, :] for r in range(rows)]
    return out


def project_kernel(rows, chips, block, me_ref, tokens_ref, cover_ref, pair_ref, tok_ref, w_ref, gains_ref, bias_ref, *refs):
    *out_refs, zn_ref, fac_ref, normed_ref, rstd_ref, left_scr, right_scr = refs
    count, chans, _ = pair_ref.shape
    gain, bias = column(gains_ref[0:1, :]), column(bias_ref[...])
    masks = mask_rows(me_ref, tokens_ref, cover_ref, tok_ref, block, rows)
    weights = jnp.concatenate([transposed(w_ref[p]) for p in range(4)], axis=0)
    for q in range(count):
        normed, rstd = layer_norm(pair_ref[q].astype(F32))
        lanes = slice(q * LANES, (q + 1) * LANES)
        normed_ref[0, :, lanes] = normed
        rstd_ref[0, :, lanes] = rstd
        zn_ref[0, :, lanes] = (normed * gain + bias).astype(BF16)
    step = 8
    for pos in range(0, count, step):
        pre = dot(weights, zn_ref[0, :, pos * LANES:(pos + step) * LANES])
        for j in range(step):
            part = pre[:, j * LANES:(j + 1) * LANES]
            pre_p = [part[p * chans:(p + 1) * chans] for p in range(4)]
            mask = masks[pos + j]
            where = pl.ds(pos + j, chans, stride=count)
            lanes = slice((pos + j) * LANES, (pos + j + 1) * LANES)
            for p, scr in ((0, left_scr), (2, right_scr)):
                sig = jax.nn.sigmoid(pre_p[p])
                sig_mask = sig * mask
                both = sig_mask * pre_p[p + 1]
                scr[where, :] = both
                fac_ref[0, p * chans:(p + 1) * chans, lanes] = both * (1.0 - sig)
                fac_ref[0, (p + 1) * chans:(p + 2) * chans, lanes] = sig_mask
    if chips:
        per = chans // chips
        for k in range(chips):
            here = pl.ds(partner_chip(me_ref, k) * (per * count), per * count)
            out_refs[k][0:per] = left_scr[here, :].astype(BF16).reshape(per, count, LANES)
            out_refs[k][per:2 * per] = right_scr[here, :].astype(BF16).reshape(per, count, LANES)
        return
    lr_ref, = out_refs
    lr_ref[:, 0] = left_scr[...].astype(BF16).reshape(chans, count, LANES)
    lr_ref[:, 1] = right_scr[...].astype(BF16).reshape(chans, count, LANES)


def prepare_kernel(block, cot_ref, zn_ref, w_ref, wo_ref, cg_ref, du_ref, dout_ref, wcat_ref, scr):
    count, chans, _ = cot_ref.shape
    wcat_ref[...] = jnp.concatenate([w_ref[0], w_ref[1], w_ref[2], w_ref[3], wo_ref[0]], axis=1)
    gates = jax.nn.sigmoid(dot(transposed(wo_ref[0]), zn_ref[0]))
    for pos in range(count):
        lanes = slice(pos * LANES, (pos + 1) * LANES)
        gate = gates[:, lanes]
        d_update = cot_ref[pos].astype(F32) * gate
        cg_ref[0, :, lanes] = d_update * (1.0 - gate)
        du_ref[0, :, lanes] = d_update.astype(BF16)
    d_outn = dot(wo_ref[1], du_ref[0])
    for pos in range(count):
        scr[pl.ds(pos, chans, stride=count), :] = d_outn[:, pos * LANES:(pos + 1) * LANES]
    dout_ref[...] = scr[...].reshape(chans, count, LANES)


def partner_chip(me_ref, k):
    return jnp.bitwise_xor(me_ref[0] // 2, k)


def collect_kernel(after_ref, *refs):
    *in_refs, out_ref = refs
    per = out_ref.shape[1]
    for k, ref in enumerate(in_refs):
        out_ref[k] = ref[per:2 * per]


def slice_rows(values, t, rows):
    chips, _, width = values.shape
    return values[:, t * rows:(t + 1) * rows].reshape(chips * rows, width).astype(BF16)


def mixed_kernel(rows, chips, me_ref, *refs):
    cols_refs, (own_ref, got_ref, out_ref, left_ref, right_ref, scr) = refs[:chips], refs[chips:]
    per, count, width = own_ref.shape[1:]
    templ, core = count // rows, me_ref[0] % 2
    for c in range(per):
        left_all = jnp.stack([ref[c].astype(F32) for ref in cols_refs])
        own, got = own_ref[:, c].astype(F32), got_ref[:, c].astype(F32)
        parts = []
        for t in range(templ):
            s = c * templ + t
            left = slice_rows(left_all, t, rows)
            left_ref[s] = left
            for k in range(chips):
                chip = partner_chip(me_ref, k)
                for values, half in ((own, core), (got, 1 - core)):
                    start = pl.multiple_of((chip * 2 + half) * rows, rows)
                    scr[s, pl.ds(start, rows), :] = values[k, t * rows:(t + 1) * rows]
            right = scr[s].astype(BF16)
            right_ref[s] = right
            parts.append(dot_nt(left, right).reshape(chips, rows, width))
        mixed = jnp.concatenate(parts, axis=1).astype(BF16)
        for k in range(chips):
            out_ref[partner_chip(me_ref, k), c] = mixed[k]


def triangle_back_kernel(rows, me_ref, dmix_ref, left_ref, right_ref, d_left_ref, keep_ref, send_ref, scr):
    chips, per, count, width = d_left_ref.shape
    templ, core = count // rows, me_ref[0] % 2
    for c in range(per):
        dmix_all = jnp.stack([dmix_ref[partner_chip(me_ref, k), c].astype(F32) for k in range(chips)])
        parts = []
        for t in range(templ):
            s = c * templ + t
            dmix = slice_rows(dmix_all, t, rows)
            parts.append(dot(dmix, right_ref[s]).reshape(chips, rows, width))
            scr[s] = dot_tn(dmix, left_ref[s])
        d_left_ref[:, c] = jnp.concatenate(parts, axis=1).astype(BF16)
    for k in range(chips):
        chip = partner_chip(me_ref, k)
        for ref, half in ((keep_ref, core), (send_ref, 1 - core)):
            here = pl.ds(pl.multiple_of((chip * 2 + half) * rows, rows), rows)
            for c in range(per):
                both = jnp.concatenate([scr[c * templ + t, here, :] for t in range(templ)], axis=0)
                ref[k, c] = both.astype(ref.dtype)


def join_kernel(d_left_ref, keep_ref, got_ref, *out_refs):
    chips, per, _, _ = d_left_ref.shape
    for k in range(chips):
        out_refs[k][0:per] = d_left_ref[k]
        out_refs[k][per:2 * per] = (keep_ref[k] + got_ref[k].astype(F32)).astype(BF16)


def split(x):
    high = x.astype(BF16).astype(F32)
    return high, x - high


def tree_sum(parts):
    while len(parts) > 1:
        parts = [a + b for a, b in zip(parts[::2], parts[1::2])] + parts[len(parts) // 2 * 2:]
    return parts[0]


def channel_sums(chans, values, scale):
    accs = [None] * 4
    for c in range(chans):
        v = values(c)
        accs[c % 4] = v if accs[c % 4] is None else [a + b for a, b in zip(accs[c % 4], v)]
    return [tree_sum(list(parts)) * scale for parts in zip(*accs)]


def middle_kernel(block, gains_ref, dout_ref, mixed_ref, dmix_ref, outn_ref, norm_ref):
    chans = dout_ref.shape[0]
    inv = 1.0 / chans

    def mixed(c):
        return mixed_ref[c].astype(F32)

    def scaled(c):
        return dout_ref[c] * gains_ref[1, c]

    mean, mean_h = channel_sums(chans, lambda c: (mixed(c), scaled(c)), inv)

    def moments(c):
        centred = mixed(c) - mean
        return centred * centred, scaled(c) * centred

    variance, mean_p = channel_sums(chans, moments, inv)
    rstd = lax.rsqrt(variance + EPS)
    mean_p = mean_p * rstd

    @pl.when(block() == 0)
    def _():
        norm_ref[...] = jnp.zeros_like(norm_ref)

    for c in range(chans):
        xhat = (mixed(c) - mean) * rstd
        outn_ref[c] = xhat * gains_ref[1, c]
        norm_ref[c:c + 1, :] += jnp.sum(dout_ref[c] * xhat, axis=0, keepdims=True)
        dmix_ref[c] = (rstd * (scaled(c) - mean_h - xhat * mean_p)).astype(BF16)


def update_kernel(block, outn_ref, norm_ref, zn_ref, cg_ref, du_ref, wo_ref, dgate_ref, grads_ref, scr, outn_scr):
    chans, count, _ = outn_ref.shape
    scr[...] = outn_ref[...].reshape(chans * count, LANES)
    for pos in range(count):
        span = slice(pos * LANES, (pos + 1) * LANES)
        outn_scr[:, span] = scr[pl.ds(pos, chans, stride=count), :].astype(BF16)
    update = dot(transposed(wo_ref[1]), outn_scr[...])
    d_gate = (cg_ref[0] * update).astype(BF16)
    dgate_ref[0] = d_gate
    gate_grad = dot_nt(zn_ref[0], d_gate)
    out_grad = dot_nt(outn_scr[...], du_ref[0])

    @pl.when(block() == 0)
    def _():
        grads_ref[...] = jnp.zeros_like(grads_ref)

    grads_ref[0:chans, 0:chans] += gate_grad
    grads_ref[0:chans, chans:2 * chans] += out_grad
    grads_ref[chans:chans + 1, 0:chans] = as_row(jnp.sum(norm_ref[...], axis=1, keepdims=True))


def gating_back_kernel(blocks, chips, block, me_ref, fac_ref, zn_ref, grads_ref, *refs):
    *in_refs, d_ref, keep_ref, send_ref, left_scr, right_scr, pack_scr = refs
    chans = zn_ref.shape[1]
    count = left_scr.shape[0] // chans
    if chips:
        per = chans // chips
        for k in range(chips):
            here = pl.ds(partner_chip(me_ref, k) * (per * count), per * count)
            left_scr[here, :] = in_refs[k][0:per].astype(F32).reshape(per * count, LANES)
            right_scr[here, :] = in_refs[k][per:2 * per].astype(F32).reshape(per * count, LANES)
    else:
        left_scr[...] = in_refs[0][:, 0].astype(F32).reshape(chans * count, LANES)
        right_scr[...] = in_refs[0][:, 1].astype(F32).reshape(chans * count, LANES)
    for pos in range(count):
        span = slice(pos * LANES, (pos + 1) * LANES)
        where = pl.ds(pos, chans, stride=count)
        d_left, d_right = left_scr[where, :], right_scr[where, :]
        for p in range(4):
            d = d_left if p < 2 else d_right
            d_ref[0, p * chans:(p + 1) * chans, span] = (d * fac_ref[0, p * chans:(p + 1) * chans, span]).astype(BF16)
    grads = dot_nt(zn_ref[0], d_ref[0])

    @pl.when(block() == 0)
    def _():
        pack_scr[...] = jnp.zeros_like(pack_scr)

    pack_scr[0:chans, :] += grads[:, 0:2 * chans]
    pack_scr[chans:2 * chans, :] += grads[:, 2 * chans:4 * chans]

    @pl.when(block() == blocks - 1)
    def _():
        for ref, half in ((keep_ref, me_ref[0] % 2), (send_ref, 1 - me_ref[0] % 2)):
            ref[0:chans, :] = pack_scr[pl.ds(pl.multiple_of(half * chans, 8), chans), :]
            ref[chans:, :] = grads_ref[pl.ds(pl.multiple_of(half * (chans // 2), 8), chans // 2), :]


def input_grad_kernel(block, d_ref, dgate_ref, normed_ref, wcat_ref, dzn_ref, norm_ref):
    chans = normed_ref.shape[1]
    d_zn = dot(wcat_ref[:, 0:4 * chans], d_ref[0]) + dot(wcat_ref[:, 4 * chans:5 * chans], dgate_ref[0])
    dzn_ref[0] = d_zn

    @pl.when(block() == 0)
    def _():
        norm_ref[...] = jnp.zeros_like(norm_ref)

    norm_ref[0:1, 0:chans] += as_row(jnp.sum(d_zn * normed_ref[0], axis=1, keepdims=True))
    norm_ref[1:2, 0:chans] += as_row(jnp.sum(d_zn, axis=1, keepdims=True))


def pair_grad_kernel(block, after_ref, dzn_ref, normed_ref, rstd_ref, gains_ref, pair_ref):
    gain = column(gains_ref[0:1, :])
    for pos in range(pair_ref.shape[0]):
        span = slice(pos * LANES, (pos + 1) * LANES)
        h = dzn_ref[0, :, span] * gain
        normed = normed_ref[0, :, span]
        mean_h = jnp.mean(h, axis=0, keepdims=True)
        mean_p = jnp.mean(h * normed, axis=0, keepdims=True)
        pair_ref[pos] = (rstd_ref[0, :, span] * (h - mean_h - normed * mean_p)).astype(BF16)


def combine_kernel(keep_ref, got_ref, norm_ref, grads_ref, out_ref):
    chans = grads_ref.shape[0] - 8
    high, low = split(jnp.concatenate([norm_ref[0:2, :], grads_ref[chans:chans + 1, :]], axis=0))
    rest = jnp.zeros((2, norm_ref.shape[1]), F32)
    block = jnp.concatenate([keep_ref[...] + got_ref[...], high, low, rest], axis=0).astype(BF16)
    for d in range(out_ref.shape[0]):
        out_ref[d] = block


def total_kernel(pack_ref, mine_ref):
    mine_ref[...] = tree_sum([pack_ref[d].astype(F32) for d in range(pack_ref.shape[0])])


def unpack_kernel(scale, me_ref, mine_ref, got_ref, proj_ref, out_ref, norms_ref):
    chans = proj_ref.shape[1]
    rows = chans + chans // 2
    odd = me_ref[0] % 2 == 1
    mine, got = mine_ref[...] * scale, got_ref[...] * scale
    for half, total in enumerate((jnp.where(odd, got, mine), jnp.where(odd, mine, got))):
        for p in range(2):
            lanes = slice(p * chans, (p + 1) * chans)
            proj_ref[2 * half + p] = total[0:chans, lanes]
            out_ref[p, half * (chans // 2):(half + 1) * (chans // 2)] = total[chans:rows, lanes]
    norm = (mine + got)[rows:rows + 6, 0:chans]
    norms_ref[...] = norm[0:3] + norm[3:6]


def exchange(x, groups=None):
    return lax.all_to_all(x, "row", split_axis=0, concat_axis=0, axis_index_groups=groups, tiled=True)


def per_device(n, pair, cotangent, token_mask, coverage, w_proj, w_out, layer_norm_gains, ln_bias):
    templ, rows, chans, width = pair.shape
    count = templ * rows
    blocks = width // LANES
    chips = n // 2
    direct = blocks == 1 and n % 2 == 0 and chips & (chips - 1) == 0 and chans % chips == 0
    per = chans // chips if direct else 1
    lanes = count * LANES
    me = lax.axis_index("row").astype(jnp.int32).reshape(1)
    tokens_row = token_mask.reshape(1, width)

    params = pltpu.CompilerParams(vmem_limit_bytes=(16 if blocks == 1 else 40) * 1024 * 1024)
    smem = pl.BlockSpec(memory_space=pltpu.SMEM)
    whole = pl.BlockSpec(memory_space=pltpu.VMEM)

    def block_spec(shape, index):
        return whole if blocks == 1 else pl.BlockSpec(shape, index)

    def full(shape):
        return block_spec(shape, lambda b: (0,) * len(shape))

    def array(shape, dtype):
        return pltpu.VMEM(shape, dtype) if blocks == 1 else jax.ShapeDtypeStruct(shape, dtype)

    def from_hbm(x):
        return pltpu.with_memory_space_constraint(x, pltpu.HBM)

    def call(name, kernel, args, in_specs, out_specs, out_shape, scratch_shapes=()):
        block = (lambda: 0) if blocks == 1 else (lambda: pl.program_id(0))
        kernel = functools.partial(kernel, block)
        return pl.pallas_call(
            kernel,
            grid=() if blocks == 1 else (blocks,),
            in_specs=in_specs,
            out_specs=out_specs,
            out_shape=out_shape,
            scratch_shapes=scratch_shapes,
            compiler_params=params,
            name=name,
        )(*args)

    rows_spec = block_spec((count, chans, LANES), lambda b: (0, 0, b))
    tok_spec = block_spec((1, LANES), lambda b: (0, b))
    lr_spec = block_spec((chans, 2, count, LANES), lambda b: (0, 0, 0, b))
    cat_spec = block_spec((1, chans, lanes), lambda b: (b, 0, 0))
    fac_spec = block_spec((1, 4 * chans, lanes), lambda b: (b, 0, 0))
    one_spec = block_spec((1, 1, lanes), lambda b: (b, 0, 0))
    chan_spec = block_spec((chans, count, LANES), lambda b: (0, 0, b))
    w_spec, wo_spec, gains_spec = full(w_proj.shape), full(w_out.shape), full(layer_norm_gains.shape)
    scratch = pltpu.VMEM((chans * count, LANES), F32)
    pair_rows = from_hbm(pair.reshape(count, chans, width))
    cot_rows = from_hbm(cotangent.reshape(count, chans, width))
    w_proj_in, w_out_in, gains_in = from_hbm(w_proj), from_hbm(w_out), from_hbm(layer_norm_gains)
    tokens_in, cover_in = from_hbm(tokens_row), from_hbm(coverage.transpose(1, 2, 0))

    def cat(dtype):
        return array((blocks, chans, lanes), dtype)

    def chunks(depth):
        return [jax.ShapeDtypeStruct((depth, count, width), BF16)] * chips

    def send_chunks(parts):
        got = [parts[0]] + [None] * (chips - 1)
        for k in reversed(range(1, chips)):
            got[k] = lax.ppermute(parts[k], "row", [(d, d ^ (2 * k)) for d in range(n)])
        return got

    *projected, zn, fac, normed, rstd = call(
        "project",
        functools.partial(project_kernel, rows, chips if direct else 0),
        (me, tokens_in, cover_in, pair_rows, tokens_in, w_proj_in, gains_in, from_hbm(ln_bias.reshape(1, chans))),
        [smem, full((1, width)), full(cover_in.shape), rows_spec, tok_spec, w_spec, gains_spec, full((1, chans))],
        ([whole] * chips if direct else [lr_spec]) + [cat_spec, fac_spec, cat_spec, one_spec],
        (chunks(2 * per) if direct else [jax.ShapeDtypeStruct((chans, 2, count, width), BF16)])
        + [cat(BF16), array((blocks, 4 * chans, lanes), F32), cat(F32), array((blocks, 1, lanes), F32)],
        [scratch, scratch],
    )
    if direct:
        cols = send_chunks(projected)

    cg, d_update, d_outn, wcat = call(
        "prepare",
        prepare_kernel,
        (cot_rows, zn, w_proj_in, w_out_in),
        [rows_spec, cat_spec, w_spec, wo_spec],
        [cat_spec, cat_spec, chan_spec, full((chans, 5 * chans))],
        [cat(F32), cat(BF16), array((chans, count, width), F32), array((chans, 5 * chans), BF16)],
        [scratch],
    )

    partner = [(d, d ^ 1) for d in range(n)]
    same_core = [list(range(core, n, 2)) for core in range(2)]
    if direct:
        slices = per * templ
        split_shape = (chips, per, count, width)
        square = pltpu.VMEM((slices, width, width), F32)
        own = pl.pallas_call(
            collect_kernel,
            in_specs=[pl.BlockSpec(memory_space=pl.ANY)] + [whole] * chips,
            out_shape=jax.ShapeDtypeStruct(split_shape, BF16),
            compiler_params=params,
            name="collect",
        )(wcat, *cols)
        got = lax.ppermute(own, "row", partner)
        mixed, left_cols, right_cols = pl.pallas_call(
            functools.partial(mixed_kernel, rows, chips),
            in_specs=[smem] + [whole] * (chips + 2),
            out_shape=[
                jax.ShapeDtypeStruct(split_shape, BF16),
                array((slices, chips * rows, width), BF16),
                array((slices, width, width), BF16),
            ],
            scratch_shapes=[square],
            compiler_params=params,
            name="mixed",
        )(me, *cols, own, got)
        mixed_rows = exchange(mixed, same_core).reshape(chans, count, width)
    else:
        slices = chans * templ // n
        cols = projected[0].reshape(chans, 2, templ, rows, width).transpose(0, 2, 1, 3, 4)
        cols = exchange(cols.reshape(n * slices, 2, rows, width)).reshape(n, slices, 2, rows, width)
        left_cols, right_cols = cols.transpose(2, 1, 0, 3, 4).reshape(2, slices, width, width)
        mixed = jnp.einsum("sik,sjk->sij", left_cols, right_cols, preferred_element_type=F32)
        mixed = mixed.astype(BF16).reshape(slices, n, rows, width).transpose(1, 0, 2, 3)
        mixed_rows = exchange(mixed.reshape(n * slices, rows, width)).reshape(chans, count, width)

    d_mixed, outn, norm_sums = call(
        "middle",
        middle_kernel,
        (layer_norm_gains, d_outn, mixed_rows),
        [smem, chan_spec, chan_spec],
        [chan_spec, chan_spec, full((chans, LANES))],
        [
            jax.ShapeDtypeStruct((chans, count, width), BF16),
            array((chans, count, width), F32),
            array((chans, LANES), F32),
        ],
    )
    if direct:
        dmix_cols = exchange(d_mixed.reshape(split_shape), same_core)

    d_gate, out_grads = call(
        "update",
        update_kernel,
        (outn, norm_sums, zn, cg, d_update, w_out),
        [chan_spec, full((chans, LANES)), cat_spec, cat_spec, cat_spec, wo_spec],
        [cat_spec, full((chans + 8, 2 * chans))],
        [cat(BF16), array((chans + 8, 2 * chans), F32)],
        [scratch, pltpu.VMEM((chans, lanes), BF16)],
    )

    if direct:
        d_left, keep, send = pl.pallas_call(
            functools.partial(triangle_back_kernel, rows),
            in_specs=[smem] + [whole] * 3,
            out_shape=[array(split_shape, BF16), array(split_shape, F32), jax.ShapeDtypeStruct(split_shape, BF16)],
            scratch_shapes=[square],
            compiler_params=params,
            name="triangle_back",
        )(me, dmix_cols, left_cols, right_cols)
        got = lax.ppermute(send, "row", partner)
        d_lr = pl.pallas_call(
            join_kernel,
            out_shape=chunks(2 * per),
            compiler_params=params,
            name="join",
        )(d_left, keep, got)
        d_lr = send_chunks(d_lr)
    else:
        dmix_cols = exchange(d_mixed.reshape(n * slices, rows, width)).reshape(n, slices, rows, width)
        dmix_cols = dmix_cols.transpose(1, 0, 2, 3).reshape(slices, width, width)
        d_left = jnp.einsum("sij,sjk->sik", dmix_cols, right_cols, preferred_element_type=F32)
        d_right = jnp.einsum("sij,sik->sjk", dmix_cols, left_cols, preferred_element_type=F32)
        d_lr = jnp.stack([d_left.astype(BF16), d_right.astype(BF16)]).reshape(2, slices, n, rows, width)
        d_lr = exchange(d_lr.transpose(2, 1, 0, 3, 4).reshape(n * slices, 2, rows, width))
        d_lr = d_lr.reshape(chans, templ, 2, rows, width).transpose(0, 2, 1, 3, 4)
        d_lr = [d_lr.reshape(chans, 2, count, width)]

    half_rows = chans + chans // 2
    d_spec = block_spec((1, 4 * chans, lanes), lambda b: (b, 0, 0))
    d_pre, keep, send = call(
        "gating_back",
        functools.partial(gating_back_kernel, blocks, chips if direct else 0),
        (me, fac, zn, out_grads, *d_lr),
        [smem, fac_spec, cat_spec, full((chans + 8, 2 * chans))] + ([whole] * chips if direct else [lr_spec]),
        [d_spec, full((half_rows, 2 * chans)), full((half_rows, 2 * chans))],
        [
            array((blocks, 4 * chans, lanes), BF16),
            array((half_rows, 2 * chans), F32),
            jax.ShapeDtypeStruct((half_rows, 2 * chans), F32),
        ],
        [scratch, scratch, pltpu.VMEM((2 * chans, 2 * chans), F32)],
    )
    got = lax.ppermute(send, "row", partner)
    d_zn, norm_rows = call(
        "input_grad",
        input_grad_kernel,
        (d_pre, d_gate, normed, wcat),
        [d_spec, cat_spec, cat_spec, full((chans, 5 * chans))],
        [cat_spec, full((8, 2 * chans))],
        [cat(F32), array((8, 2 * chans), F32)],
    )
    sums = pl.pallas_call(
        combine_kernel,
        out_shape=jax.ShapeDtypeStruct((chips, half_rows + 8, 2 * chans), BF16),
        compiler_params=params,
        name="combine",
    )(keep, got, norm_rows, out_grads)
    sums = exchange(sums, same_core)
    mine = pl.pallas_call(
        total_kernel,
        out_shape=jax.ShapeDtypeStruct((half_rows + 8, 2 * chans), F32),
        compiler_params=params,
        name="total",
    )(sums)
    got = lax.ppermute(mine, "row", partner)
    pair_grad = call(
        "pair_grad",
        pair_grad_kernel,
        (mine, d_zn, normed, rstd, layer_norm_gains),
        [pl.BlockSpec(memory_space=pl.ANY), cat_spec, cat_spec, one_spec, gains_spec],
        rows_spec,
        jax.ShapeDtypeStruct((count, chans, width), BF16),
    )
    grad_proj, grad_out, norm_grads = pl.pallas_call(
        functools.partial(unpack_kernel, 1.0 / width),
        in_specs=[smem] + [whole] * 2,
        out_shape=[
            jax.ShapeDtypeStruct(w_proj.shape, F32),
            jax.ShapeDtypeStruct(w_out.shape, F32),
            jax.ShapeDtypeStruct((3, chans), F32),
        ],
        compiler_params=params,
        name="unpack",
    )(me, mine, got)
    return pair_grad.reshape(pair.shape), grad_proj, grad_out, norm_grads


def solution(mesh):
    return jax.shard_map(
        functools.partial(per_device, mesh.shape["row"]),
        mesh=mesh,
        in_specs=(
            P("groups", "row", None, None),
            P("groups", "row", None, None),
            P("groups"),
            P("groups", None, None),
            P(),
            P(),
            P(),
            P(),
        ),
        out_specs=(
            P("groups", "row", None, None),
            P("groups", None, None),
            P("groups", None, None),
            P("groups", None),
        ),
        check_vma=False,
    )
```

```python
import functools

import jax
import jax.numpy as jnp
from jax import lax
from jax.experimental import pallas as pl
from jax.experimental.pallas import tpu as pltpu
from jax.sharding import PartitionSpec as P

EPS = 1e-05
LANES = 128
F32 = jnp.float32
BF16 = jnp.bfloat16


def dot(a, b):
    return jnp.dot(a, b, preferred_element_type=F32)


def dot_nt(a, b):
    return lax.dot_general(a, b, (((1,), (1,)), ((), ())), preferred_element_type=F32)


def dot_tn(a, b):
    return lax.dot_general(a, b, (((0,), (0,)), ((), ())), preferred_element_type=F32)


def transposed(weight):
    return weight.astype(F32).T.astype(BF16)


def column(row):
    n = row.shape[1]
    eye = lax.broadcasted_iota(jnp.int32, (n, n), 0) == lax.broadcasted_iota(jnp.int32, (n, n), 1)
    return jnp.sum(jnp.where(eye, row, 0.0), axis=1, keepdims=True)


def as_row(col):
    n = col.shape[0]
    eye = lax.broadcasted_iota(jnp.int32, (n, n), 0) == lax.broadcasted_iota(jnp.int32, (n, n), 1)
    return jnp.sum(jnp.where(eye, col, 0.0), axis=0, keepdims=True)


def layer_norm(x):
    mean = jnp.mean(x, axis=0, keepdims=True)
    centred = x - mean
    rstd = lax.rsqrt(jnp.mean(centred * centred, axis=0, keepdims=True) + EPS)
    return centred * rstd, rstd


def mask_rows(me_ref, tokens_ref, cover_ref, tok_ref, block, rows):
    width, (tiles, _, templ) = tokens_ref.shape[1], cover_ref.shape
    tile = width // tiles
    first = me_ref[0] * rows
    here = lax.broadcasted_iota(jnp.int32, (rows, width), 0) + first == lax.broadcasted_iota(jnp.int32, (rows, width), 1)
    row_mask = jnp.sum(jnp.where(here, tokens_ref[...].astype(F32), 0.0), axis=1, keepdims=True)
    column_mask = tok_ref[...].astype(F32)
    cover = cover_ref[first // tile].astype(F32)
    here = lax.broadcasted_iota(jnp.int32, (tiles, templ), 0) == block() * LANES // tile
    cover = jnp.sum(jnp.where(here, cover, 0.0), axis=0, keepdims=True)
    out = []
    for t in range(templ):
        masked = column_mask * cover[:, t:t + 1]
        out += [masked * row_mask[r:r + 1, :] for r in range(rows)]
    return out


def project_kernel(rows, chips, block, me_ref, tokens_ref, cover_ref, pair_ref, tok_ref, w_ref, gains_ref, bias_ref, *refs):
    *out_refs, zn_ref, fac_ref, normed_ref, rstd_ref, left_scr, right_scr = refs
    count, chans, _ = pair_ref.shape
    gain, bias = column(gains_ref[0:1, :]), column(bias_ref[...])
    masks = mask_rows(me_ref, tokens_ref, cover_ref, tok_ref, block, rows)
    weights = jnp.concatenate([transposed(w_ref[p]) for p in range(4)], axis=0)
    for q in range(count):
        normed, rstd = layer_norm(pair_ref[q].astype(F32))
        lanes = slice(q * LANES, (q + 1) * LANES)
        normed_ref[0, :, lanes] = normed
        rstd_ref[0, :, lanes] = rstd
        zn_ref[0, :, lanes] = (normed * gain + bias).astype(BF16)
    step = 8
    for pos in range(0, count, step):
        pre = dot(weights, zn_ref[0, :, pos * LANES:(pos + step) * LANES])
        for j in range(step):
            part = pre[:, j * LANES:(j + 1) * LANES]
            pre_p = [part[p * chans:(p + 1) * chans] for p in range(4)]
            mask = masks[pos + j]
            where = pl.ds(pos + j, chans, stride=count)
            lanes = slice((pos + j) * LANES, (pos + j + 1) * LANES)
            for p, scr in ((0, left_scr), (2, right_scr)):
                sig = jax.nn.sigmoid(pre_p[p])
                sig_mask = sig * mask
                both = sig_mask * pre_p[p + 1]
                scr[where, :] = both
                fac_ref[0, p * chans:(p + 1) * chans, lanes] = both * (1.0 - sig)
                fac_ref[0, (p + 1) * chans:(p + 2) * chans, lanes] = sig_mask
    if chips:
        per = chans // chips
        for k in range(chips):
            here = pl.ds(chunk_chip(me_ref, k, chips) * (per * count), per * count)
            out_refs[k][0:per] = left_scr[here, :].astype(BF16).reshape(per, count, LANES)
            out_refs[k][per:2 * per] = right_scr[here, :].astype(BF16).reshape(per, count, LANES)
        return
    lr_ref, = out_refs
    lr_ref[:, 0] = left_scr[...].astype(BF16).reshape(chans, count, LANES)
    lr_ref[:, 1] = right_scr[...].astype(BF16).reshape(chans, count, LANES)


def prepare_kernel(block, cot_ref, zn_ref, w_ref, wo_ref, cg_ref, du_ref, dout_ref, wcat_ref, scr):
    count, chans, _ = cot_ref.shape
    wcat_ref[...] = jnp.concatenate([w_ref[0], w_ref[1], w_ref[2], w_ref[3], wo_ref[0]], axis=1)
    gates = jax.nn.sigmoid(dot(transposed(wo_ref[0]), zn_ref[0]))
    for pos in range(count):
        lanes = slice(pos * LANES, (pos + 1) * LANES)
        gate = gates[:, lanes]
        d_update = cot_ref[pos].astype(F32) * gate
        cg_ref[0, :, lanes] = d_update * (1.0 - gate)
        du_ref[0, :, lanes] = d_update.astype(BF16)
    d_outn = dot(wo_ref[1], du_ref[0])
    for pos in range(count):
        scr[pl.ds(pos, chans, stride=count), :] = d_outn[:, pos * LANES:(pos + 1) * LANES]
    dout_ref[...] = scr[...].reshape(chans, count, LANES)


def chunk_order(chips):
    half = chips // 2
    far = [half + (j ^ (half // 2)) for j in range(half)]
    near = list(range(1, half))
    return [step for pair in zip(far, near) for step in pair] + far[len(near):] + [0]


def chunk_chip(me_ref, k, chips):
    return jnp.bitwise_xor(me_ref[0] // 2, chunk_order(chips)[k])


def collect_kernel(after_ref, *refs):
    *in_refs, out_ref = refs
    per = out_ref.shape[1]
    for k, ref in enumerate(in_refs):
        out_ref[k] = ref[per:2 * per]


def slice_rows(values, t, rows):
    chips, _, width = values.shape
    return values[:, t * rows:(t + 1) * rows].reshape(chips * rows, width).astype(BF16)


def mixed_kernel(rows, chips, me_ref, *refs):
    cols_refs, (own_ref, got_ref, out_ref, left_ref, right_ref, scr) = refs[:chips], refs[chips:]
    per, count, width = own_ref.shape[1:]
    templ, core = count // rows, me_ref[0] % 2
    for c in range(per):
        left_all = jnp.stack([ref[c].astype(F32) for ref in cols_refs])
        own, got = own_ref[:, c].astype(F32), got_ref[:, c].astype(F32)
        parts = []
        for t in range(templ):
            s = c * templ + t
            left = slice_rows(left_all, t, rows)
            left_ref[s] = left
            for k in range(chips):
                chip = chunk_chip(me_ref, k, chips)
                for values, half in ((own, core), (got, 1 - core)):
                    start = pl.multiple_of((chip * 2 + half) * rows, rows)
                    scr[s, pl.ds(start, rows), :] = values[k, t * rows:(t + 1) * rows]
            right = scr[s].astype(BF16)
            right_ref[s] = right
            parts.append(dot_nt(left, right).reshape(chips, rows, width))
        mixed = jnp.concatenate(parts, axis=1).astype(BF16)
        for k in range(chips):
            out_ref[chunk_chip(me_ref, k, chips), c] = mixed[k]


def triangle_back_kernel(rows, me_ref, dmix_ref, left_ref, right_ref, d_left_ref, keep_ref, send_ref, scr):
    chips, per, count, width = d_left_ref.shape
    templ, core = count // rows, me_ref[0] % 2
    for c in range(per):
        dmix_all = jnp.stack([dmix_ref[chunk_chip(me_ref, k, chips), c].astype(F32) for k in range(chips)])
        parts = []
        for t in range(templ):
            s = c * templ + t
            dmix = slice_rows(dmix_all, t, rows)
            parts.append(dot(dmix, right_ref[s]).reshape(chips, rows, width))
            scr[s] = dot_tn(dmix, left_ref[s])
        d_left_ref[:, c] = jnp.concatenate(parts, axis=1).astype(BF16)
    for k in range(chips):
        chip = chunk_chip(me_ref, k, chips)
        for ref, half in ((keep_ref, core), (send_ref, 1 - core)):
            here = pl.ds(pl.multiple_of((chip * 2 + half) * rows, rows), rows)
            for c in range(per):
                both = jnp.concatenate([scr[c * templ + t, here, :] for t in range(templ)], axis=0)
                ref[k, c] = both.astype(ref.dtype)


def join_kernel(d_left_ref, keep_ref, got_ref, *out_refs):
    chips, per, _, _ = d_left_ref.shape
    for k in range(chips):
        out_refs[k][0:per] = d_left_ref[k]
        out_refs[k][per:2 * per] = (keep_ref[k] + got_ref[k].astype(F32)).astype(BF16)


def split(x):
    high = x.astype(BF16).astype(F32)
    return high, x - high


def tree_sum(parts):
    while len(parts) > 1:
        parts = [a + b for a, b in zip(parts[::2], parts[1::2])] + parts[len(parts) // 2 * 2:]
    return parts[0]


def channel_sums(chans, values, scale):
    accs = [None] * 4
    for c in range(chans):
        v = values(c)
        accs[c % 4] = v if accs[c % 4] is None else [a + b for a, b in zip(accs[c % 4], v)]
    return [tree_sum(list(parts)) * scale for parts in zip(*accs)]


def middle_kernel(block, gains_ref, dout_ref, mixed_ref, dmix_ref, outn_ref, norm_ref):
    chans = dout_ref.shape[0]
    inv = 1.0 / chans

    def mixed(c):
        return mixed_ref[c].astype(F32)

    def scaled(c):
        return dout_ref[c] * gains_ref[1, c]

    mean, mean_h = channel_sums(chans, lambda c: (mixed(c), scaled(c)), inv)

    def moments(c):
        centred = mixed(c) - mean
        return centred * centred, scaled(c) * centred

    variance, mean_p = channel_sums(chans, moments, inv)
    rstd = lax.rsqrt(variance + EPS)
    mean_p = mean_p * rstd

    @pl.when(block() == 0)
    def _():
        norm_ref[...] = jnp.zeros_like(norm_ref)

    for c in range(chans):
        xhat = (mixed(c) - mean) * rstd
        outn_ref[c] = xhat * gains_ref[1, c]
        norm_ref[c:c + 1, :] += jnp.sum(dout_ref[c] * xhat, axis=0, keepdims=True)
        dmix_ref[c] = (rstd * (scaled(c) - mean_h - xhat * mean_p)).astype(BF16)


def update_kernel(block, outn_ref, norm_ref, zn_ref, cg_ref, du_ref, wo_ref, dgate_ref, grads_ref, scr, outn_scr):
    chans, count, _ = outn_ref.shape
    scr[...] = outn_ref[...].reshape(chans * count, LANES)
    for pos in range(count):
        span = slice(pos * LANES, (pos + 1) * LANES)
        outn_scr[:, span] = scr[pl.ds(pos, chans, stride=count), :].astype(BF16)
    update = dot(transposed(wo_ref[1]), outn_scr[...])
    d_gate = (cg_ref[0] * update).astype(BF16)
    dgate_ref[0] = d_gate
    gate_grad = dot_nt(zn_ref[0], d_gate)
    out_grad = dot_nt(outn_scr[...], du_ref[0])

    @pl.when(block() == 0)
    def _():
        grads_ref[...] = jnp.zeros_like(grads_ref)

    grads_ref[0:chans, 0:chans] += gate_grad
    grads_ref[0:chans, chans:2 * chans] += out_grad
    grads_ref[chans:chans + 1, 0:chans] = as_row(jnp.sum(norm_ref[...], axis=1, keepdims=True))


def gating_back_kernel(blocks, chips, block, me_ref, fac_ref, zn_ref, grads_ref, *refs):
    *in_refs, d_ref, keep_ref, send_ref, left_scr, right_scr, pack_scr = refs
    chans = zn_ref.shape[1]
    count = left_scr.shape[0] // chans
    if chips:
        per = chans // chips
        for k in range(chips):
            here = pl.ds(chunk_chip(me_ref, k, chips) * (per * count), per * count)
            left_scr[here, :] = in_refs[k][0:per].astype(F32).reshape(per * count, LANES)
            right_scr[here, :] = in_refs[k][per:2 * per].astype(F32).reshape(per * count, LANES)
    else:
        left_scr[...] = in_refs[0][:, 0].astype(F32).reshape(chans * count, LANES)
        right_scr[...] = in_refs[0][:, 1].astype(F32).reshape(chans * count, LANES)
    for pos in range(count):
        span = slice(pos * LANES, (pos + 1) * LANES)
        where = pl.ds(pos, chans, stride=count)
        d_left, d_right = left_scr[where, :], right_scr[where, :]
        for p in range(4):
            d = d_left if p < 2 else d_right
            d_ref[0, p * chans:(p + 1) * chans, span] = (d * fac_ref[0, p * chans:(p + 1) * chans, span]).astype(BF16)
    grads = dot_nt(zn_ref[0], d_ref[0])

    @pl.when(block() == 0)
    def _():
        pack_scr[...] = jnp.zeros_like(pack_scr)

    pack_scr[0:chans, :] += grads[:, 0:2 * chans]
    pack_scr[chans:2 * chans, :] += grads[:, 2 * chans:4 * chans]

    @pl.when(block() == blocks - 1)
    def _():
        for ref, half in ((keep_ref, me_ref[0] % 2), (send_ref, 1 - me_ref[0] % 2)):
            ref[0:chans, :] = pack_scr[pl.ds(pl.multiple_of(half * chans, 8), chans), :]
            ref[chans:, :] = grads_ref[pl.ds(pl.multiple_of(half * (chans // 2), 8), chans // 2), :]


def input_grad_kernel(block, d_ref, dgate_ref, normed_ref, wcat_ref, dzn_ref, norm_ref):
    chans = normed_ref.shape[1]
    d_zn = dot(wcat_ref[:, 0:4 * chans], d_ref[0]) + dot(wcat_ref[:, 4 * chans:5 * chans], dgate_ref[0])
    dzn_ref[0] = d_zn

    @pl.when(block() == 0)
    def _():
        norm_ref[...] = jnp.zeros_like(norm_ref)

    norm_ref[0:1, 0:chans] += as_row(jnp.sum(d_zn * normed_ref[0], axis=1, keepdims=True))
    norm_ref[1:2, 0:chans] += as_row(jnp.sum(d_zn, axis=1, keepdims=True))


def pair_grad_kernel(block, after_ref, dzn_ref, normed_ref, rstd_ref, gains_ref, pair_ref):
    gain = column(gains_ref[0:1, :])
    for pos in range(pair_ref.shape[0]):
        span = slice(pos * LANES, (pos + 1) * LANES)
        h = dzn_ref[0, :, span] * gain
        normed = normed_ref[0, :, span]
        mean_h = jnp.mean(h, axis=0, keepdims=True)
        mean_p = jnp.mean(h * normed, axis=0, keepdims=True)
        pair_ref[pos] = (rstd_ref[0, :, span] * (h - mean_h - normed * mean_p)).astype(BF16)


def combine_kernel(keep_ref, got_ref, norm_ref, grads_ref, out_ref):
    chans = grads_ref.shape[0] - 8
    high, low = split(jnp.concatenate([norm_ref[0:2, :], grads_ref[chans:chans + 1, :]], axis=0))
    rest = jnp.zeros((2, norm_ref.shape[1]), F32)
    block = jnp.concatenate([keep_ref[...] + got_ref[...], high, low, rest], axis=0).astype(BF16)
    for d in range(out_ref.shape[0]):
        out_ref[d] = block


def total_kernel(pack_ref, mine_ref):
    mine_ref[...] = tree_sum([pack_ref[d].astype(F32) for d in range(pack_ref.shape[0])])


def unpack_kernel(scale, me_ref, mine_ref, got_ref, proj_ref, out_ref, norms_ref):
    chans = proj_ref.shape[1]
    rows = chans + chans // 2
    odd = me_ref[0] % 2 == 1
    mine, got = mine_ref[...] * scale, got_ref[...] * scale
    for half, total in enumerate((jnp.where(odd, got, mine), jnp.where(odd, mine, got))):
        for p in range(2):
            lanes = slice(p * chans, (p + 1) * chans)
            proj_ref[2 * half + p] = total[0:chans, lanes]
            out_ref[p, half * (chans // 2):(half + 1) * (chans // 2)] = total[chans:rows, lanes]
    norm = (mine + got)[rows:rows + 6, 0:chans]
    norms_ref[...] = norm[0:3] + norm[3:6]


def exchange(x, groups=None):
    return lax.all_to_all(x, "row", split_axis=0, concat_axis=0, axis_index_groups=groups, tiled=True)


def per_device(n, pair, cotangent, token_mask, coverage, w_proj, w_out, layer_norm_gains, ln_bias):
    templ, rows, chans, width = pair.shape
    count = templ * rows
    blocks = width // LANES
    chips = n // 2
    direct = blocks == 1 and n % 2 == 0 and chips & (chips - 1) == 0 and chans % chips == 0
    per = chans // chips if direct else 1
    lanes = count * LANES
    me = lax.axis_index("row").astype(jnp.int32).reshape(1)
    tokens_row = token_mask.reshape(1, width)

    params = pltpu.CompilerParams(vmem_limit_bytes=(16 if blocks == 1 else 40) * 1024 * 1024)
    smem = pl.BlockSpec(memory_space=pltpu.SMEM)
    whole = pl.BlockSpec(memory_space=pltpu.VMEM)

    def block_spec(shape, index):
        return whole if blocks == 1 else pl.BlockSpec(shape, index)

    def full(shape):
        return block_spec(shape, lambda b: (0,) * len(shape))

    def array(shape, dtype):
        return pltpu.VMEM(shape, dtype) if blocks == 1 else jax.ShapeDtypeStruct(shape, dtype)

    def from_hbm(x):
        return pltpu.with_memory_space_constraint(x, pltpu.HBM)

    def call(name, kernel, args, in_specs, out_specs, out_shape, scratch_shapes=()):
        block = (lambda: 0) if blocks == 1 else (lambda: pl.program_id(0))
        kernel = functools.partial(kernel, block)
        return pl.pallas_call(
            kernel,
            grid=() if blocks == 1 else (blocks,),
            in_specs=in_specs,
            out_specs=out_specs,
            out_shape=out_shape,
            scratch_shapes=scratch_shapes,
            compiler_params=params,
            name=name,
        )(*args)

    rows_spec = block_spec((count, chans, LANES), lambda b: (0, 0, b))
    tok_spec = block_spec((1, LANES), lambda b: (0, b))
    lr_spec = block_spec((chans, 2, count, LANES), lambda b: (0, 0, 0, b))
    cat_spec = block_spec((1, chans, lanes), lambda b: (b, 0, 0))
    fac_spec = block_spec((1, 4 * chans, lanes), lambda b: (b, 0, 0))
    one_spec = block_spec((1, 1, lanes), lambda b: (b, 0, 0))
    chan_spec = block_spec((chans, count, LANES), lambda b: (0, 0, b))
    w_spec, wo_spec, gains_spec = full(w_proj.shape), full(w_out.shape), full(layer_norm_gains.shape)
    scratch = pltpu.VMEM((chans * count, LANES), F32)
    pair_rows = from_hbm(pair.reshape(count, chans, width))
    cot_rows = from_hbm(cotangent.reshape(count, chans, width))
    w_proj_in, w_out_in, gains_in = from_hbm(w_proj), from_hbm(w_out), from_hbm(layer_norm_gains)
    tokens_in, cover_in = from_hbm(tokens_row), from_hbm(coverage.transpose(1, 2, 0))

    def cat(dtype):
        return array((blocks, chans, lanes), dtype)

    def chunks(depth):
        return [jax.ShapeDtypeStruct((depth, count, width), BF16)] * chips

    def send_chunks(parts):
        return [
            lax.ppermute(part, "row", [(d, d ^ (2 * step)) for d in range(n)]) if step else part
            for part, step in zip(parts, chunk_order(chips))
        ]

    *projected, zn, fac, normed, rstd = call(
        "project",
        functools.partial(project_kernel, rows, chips if direct else 0),
        (me, tokens_in, cover_in, pair_rows, tokens_in, w_proj_in, gains_in, from_hbm(ln_bias.reshape(1, chans))),
        [smem, full((1, width)), full(cover_in.shape), rows_spec, tok_spec, w_spec, gains_spec, full((1, chans))],
        ([whole] * chips if direct else [lr_spec]) + [cat_spec, fac_spec, cat_spec, one_spec],
        (chunks(2 * per) if direct else [jax.ShapeDtypeStruct((chans, 2, count, width), BF16)])
        + [cat(BF16), array((blocks, 4 * chans, lanes), F32), cat(F32), array((blocks, 1, lanes), F32)],
        [scratch, scratch],
    )
    if direct:
        cols = send_chunks(projected)

    cg, d_update, d_outn, wcat = call(
        "prepare",
        prepare_kernel,
        (cot_rows, zn, w_proj_in, w_out_in),
        [rows_spec, cat_spec, w_spec, wo_spec],
        [cat_spec, cat_spec, chan_spec, full((chans, 5 * chans))],
        [cat(F32), cat(BF16), array((chans, count, width), F32), array((chans, 5 * chans), BF16)],
        [scratch],
    )

    partner = [(d, d ^ 1) for d in range(n)]
    same_core = [list(range(core, n, 2)) for core in range(2)]
    if direct:
        slices = per * templ
        split_shape = (chips, per, count, width)
        square = pltpu.VMEM((slices, width, width), F32)
        own = pl.pallas_call(
            collect_kernel,
            in_specs=[pl.BlockSpec(memory_space=pl.ANY)] + [whole] * chips,
            out_shape=jax.ShapeDtypeStruct(split_shape, BF16),
            compiler_params=params,
            name="collect",
        )(wcat, *cols)
        got = lax.ppermute(own, "row", partner)
        mixed, left_cols, right_cols = pl.pallas_call(
            functools.partial(mixed_kernel, rows, chips),
            in_specs=[smem] + [whole] * (chips + 2),
            out_shape=[
                jax.ShapeDtypeStruct(split_shape, BF16),
                array((slices, chips * rows, width), BF16),
                array((slices, width, width), BF16),
            ],
            scratch_shapes=[square],
            compiler_params=params,
            name="mixed",
        )(me, *cols, own, got)
        mixed_rows = exchange(mixed, same_core).reshape(chans, count, width)
    else:
        slices = chans * templ // n
        cols = projected[0].reshape(chans, 2, templ, rows, width).transpose(0, 2, 1, 3, 4)
        cols = exchange(cols.reshape(n * slices, 2, rows, width)).reshape(n, slices, 2, rows, width)
        left_cols, right_cols = cols.transpose(2, 1, 0, 3, 4).reshape(2, slices, width, width)
        mixed = jnp.einsum("sik,sjk->sij", left_cols, right_cols, preferred_element_type=F32)
        mixed = mixed.astype(BF16).reshape(slices, n, rows, width).transpose(1, 0, 2, 3)
        mixed_rows = exchange(mixed.reshape(n * slices, rows, width)).reshape(chans, count, width)

    d_mixed, outn, norm_sums = call(
        "middle",
        middle_kernel,
        (layer_norm_gains, d_outn, mixed_rows),
        [smem, chan_spec, chan_spec],
        [chan_spec, chan_spec, full((chans, LANES))],
        [
            jax.ShapeDtypeStruct((chans, count, width), BF16),
            array((chans, count, width), F32),
            array((chans, LANES), F32),
        ],
    )
    if direct:
        dmix_cols = exchange(d_mixed.reshape(split_shape), same_core)

    d_gate, out_grads = call(
        "update",
        update_kernel,
        (outn, norm_sums, zn, cg, d_update, w_out),
        [chan_spec, full((chans, LANES)), cat_spec, cat_spec, cat_spec, wo_spec],
        [cat_spec, full((chans + 8, 2 * chans))],
        [cat(BF16), array((chans + 8, 2 * chans), F32)],
        [scratch, pltpu.VMEM((chans, lanes), BF16)],
    )

    if direct:
        d_left, keep, send = pl.pallas_call(
            functools.partial(triangle_back_kernel, rows),
            in_specs=[smem] + [whole] * 3,
            out_shape=[array(split_shape, BF16), array(split_shape, F32), jax.ShapeDtypeStruct(split_shape, BF16)],
            scratch_shapes=[square],
            compiler_params=params,
            name="triangle_back",
        )(me, dmix_cols, left_cols, right_cols)
        got = lax.ppermute(send, "row", partner)
        d_lr = pl.pallas_call(
            join_kernel,
            out_shape=chunks(2 * per),
            compiler_params=params,
            name="join",
        )(d_left, keep, got)
        d_lr = send_chunks(d_lr)
    else:
        dmix_cols = exchange(d_mixed.reshape(n * slices, rows, width)).reshape(n, slices, rows, width)
        dmix_cols = dmix_cols.transpose(1, 0, 2, 3).reshape(slices, width, width)
        d_left = jnp.einsum("sij,sjk->sik", dmix_cols, right_cols, preferred_element_type=F32)
        d_right = jnp.einsum("sij,sik->sjk", dmix_cols, left_cols, preferred_element_type=F32)
        d_lr = jnp.stack([d_left.astype(BF16), d_right.astype(BF16)]).reshape(2, slices, n, rows, width)
        d_lr = exchange(d_lr.transpose(2, 1, 0, 3, 4).reshape(n * slices, 2, rows, width))
        d_lr = d_lr.reshape(chans, templ, 2, rows, width).transpose(0, 2, 1, 3, 4)
        d_lr = [d_lr.reshape(chans, 2, count, width)]

    half_rows = chans + chans // 2
    d_spec = block_spec((1, 4 * chans, lanes), lambda b: (b, 0, 0))
    d_pre, keep, send = call(
        "gating_back",
        functools.partial(gating_back_kernel, blocks, chips if direct else 0),
        (me, fac, zn, out_grads, *d_lr),
        [smem, fac_spec, cat_spec, full((chans + 8, 2 * chans))] + ([whole] * chips if direct else [lr_spec]),
        [d_spec, full((half_rows, 2 * chans)), full((half_rows, 2 * chans))],
        [
            array((blocks, 4 * chans, lanes), BF16),
            array((half_rows, 2 * chans), F32),
            jax.ShapeDtypeStruct((half_rows, 2 * chans), F32),
        ],
        [scratch, scratch, pltpu.VMEM((2 * chans, 2 * chans), F32)],
    )
    got = lax.ppermute(send, "row", partner)
    d_zn, norm_rows = call(
        "input_grad",
        input_grad_kernel,
        (d_pre, d_gate, normed, wcat),
        [d_spec, cat_spec, cat_spec, full((chans, 5 * chans))],
        [cat_spec, full((8, 2 * chans))],
        [cat(F32), array((8, 2 * chans), F32)],
    )
    sums = pl.pallas_call(
        combine_kernel,
        out_shape=jax.ShapeDtypeStruct((chips, half_rows + 8, 2 * chans), BF16),
        compiler_params=params,
        name="combine",
    )(keep, got, norm_rows, out_grads)
    sums = exchange(sums, same_core)
    mine = pl.pallas_call(
        total_kernel,
        out_shape=jax.ShapeDtypeStruct((half_rows + 8, 2 * chans), F32),
        compiler_params=params,
        name="total",
    )(sums)
    got = lax.ppermute(mine, "row", partner)
    pair_grad = call(
        "pair_grad",
        pair_grad_kernel,
        (mine, d_zn, normed, rstd, layer_norm_gains),
        [pl.BlockSpec(memory_space=pl.ANY), cat_spec, cat_spec, one_spec, gains_spec],
        rows_spec,
        jax.ShapeDtypeStruct((count, chans, width), BF16),
    )
    grad_proj, grad_out, norm_grads = pl.pallas_call(
        functools.partial(unpack_kernel, 1.0 / width),
        in_specs=[smem] + [whole] * 2,
        out_shape=[
            jax.ShapeDtypeStruct(w_proj.shape, F32),
            jax.ShapeDtypeStruct(w_out.shape, F32),
            jax.ShapeDtypeStruct((3, chans), F32),
        ],
        compiler_params=params,
        name="unpack",
    )(me, mine, got)
    return pair_grad.reshape(pair.shape), grad_proj, grad_out, norm_grads


def solution(mesh):
    return jax.shard_map(
        functools.partial(per_device, mesh.shape["row"]),
        mesh=mesh,
        in_specs=(
            P("groups", "row", None, None),
            P("groups", "row", None, None),
            P("groups"),
            P("groups", None, None),
            P(),
            P(),
            P(),
            P(),
        ),
        out_specs=(
            P("groups", "row", None, None),
            P("groups", None, None),
            P("groups", None, None),
            P("groups", None),
        ),
        check_vma=False,
    )
```

```python
import functools

import jax
import jax.numpy as jnp
from jax import lax
from jax.experimental import pallas as pl
from jax.experimental.pallas import tpu as pltpu
from jax.sharding import PartitionSpec as P

EPS = 1e-05
LANES = 128
F32 = jnp.float32
BF16 = jnp.bfloat16


def dot(a, b):
    return jnp.dot(a, b, preferred_element_type=F32)


def dot_nt(a, b):
    return lax.dot_general(a, b, (((1,), (1,)), ((), ())), preferred_element_type=F32)


def dot_tn(a, b):
    return lax.dot_general(a, b, (((0,), (0,)), ((), ())), preferred_element_type=F32)


def transposed(weight):
    return weight.astype(F32).T.astype(BF16)


def column(row):
    n = row.shape[1]
    eye = lax.broadcasted_iota(jnp.int32, (n, n), 0) == lax.broadcasted_iota(jnp.int32, (n, n), 1)
    return jnp.sum(jnp.where(eye, row, 0.0), axis=1, keepdims=True)


def as_row(col):
    n = col.shape[0]
    eye = lax.broadcasted_iota(jnp.int32, (n, n), 0) == lax.broadcasted_iota(jnp.int32, (n, n), 1)
    return jnp.sum(jnp.where(eye, col, 0.0), axis=0, keepdims=True)


def layer_norm(x):
    mean = jnp.mean(x, axis=0, keepdims=True)
    centred = x - mean
    rstd = lax.rsqrt(jnp.mean(centred * centred, axis=0, keepdims=True) + EPS)
    return centred * rstd, rstd


def mask_rows(me_ref, tokens_ref, cover_ref, tok_ref, block, rows):
    width, (tiles, _, templ) = tokens_ref.shape[1], cover_ref.shape
    tile = width // tiles
    first = me_ref[0] * rows
    here = lax.broadcasted_iota(jnp.int32, (rows, width), 0) + first == lax.broadcasted_iota(jnp.int32, (rows, width), 1)
    row_mask = jnp.sum(jnp.where(here, tokens_ref[...].astype(F32), 0.0), axis=1, keepdims=True)
    column_mask = tok_ref[...].astype(F32)
    cover = cover_ref[first // tile].astype(F32)
    here = lax.broadcasted_iota(jnp.int32, (tiles, templ), 0) == block() * LANES // tile
    cover = jnp.sum(jnp.where(here, cover, 0.0), axis=0, keepdims=True)
    out = []
    for t in range(templ):
        masked = column_mask * cover[:, t:t + 1]
        out += [masked * row_mask[r:r + 1, :] for r in range(rows)]
    return out


def project_kernel(rows, chips, block, me_ref, tokens_ref, cover_ref, pair_ref, tok_ref, w_ref, gains_ref, bias_ref, *refs):
    *out_refs, zn_ref, fac_ref, normed_ref, rstd_ref, left_scr, right_scr = refs
    count, chans, _ = pair_ref.shape
    gain, bias = column(gains_ref[0:1, :]), column(bias_ref[...])
    masks = mask_rows(me_ref, tokens_ref, cover_ref, tok_ref, block, rows)
    weights = jnp.concatenate([transposed(w_ref[p]) for p in range(4)], axis=0)
    for q in range(count):
        normed, rstd = layer_norm(pair_ref[q].astype(F32))
        lanes = slice(q * LANES, (q + 1) * LANES)
        normed_ref[0, :, lanes] = normed
        rstd_ref[0, :, lanes] = rstd
        zn_ref[0, :, lanes] = (normed * gain + bias).astype(BF16)
    step = 8
    for pos in range(0, count, step):
        pre = dot(weights, zn_ref[0, :, pos * LANES:(pos + step) * LANES])
        for j in range(step):
            part = pre[:, j * LANES:(j + 1) * LANES]
            pre_p = [part[p * chans:(p + 1) * chans] for p in range(4)]
            mask = masks[pos + j]
            where = pl.ds(pos + j, chans, stride=count)
            lanes = slice((pos + j) * LANES, (pos + j + 1) * LANES)
            for p, scr in ((0, left_scr), (2, right_scr)):
                sig = jax.nn.sigmoid(pre_p[p])
                sig_mask = sig * mask
                both = sig_mask * pre_p[p + 1]
                scr[where, :] = both
                fac_ref[0, p * chans:(p + 1) * chans, lanes] = both * (1.0 - sig)
                fac_ref[0, (p + 1) * chans:(p + 2) * chans, lanes] = sig_mask
    if chips:
        per = chans // chips
        for k in range(chips):
            here = pl.ds(chunk_chip(me_ref, k, chips) * (per * count), per * count)
            out_refs[k][0:per] = left_scr[here, :].astype(BF16).reshape(per, count, LANES)
            out_refs[k][per:2 * per] = right_scr[here, :].astype(BF16).reshape(per, count, LANES)
        return
    lr_ref, = out_refs
    lr_ref[:, 0] = left_scr[...].astype(BF16).reshape(chans, count, LANES)
    lr_ref[:, 1] = right_scr[...].astype(BF16).reshape(chans, count, LANES)


def prepare_kernel(block, cot_ref, zn_ref, w_ref, wo_ref, cg_ref, du_ref, dout_ref, wcat_ref, scr):
    count, chans, _ = cot_ref.shape
    wcat_ref[...] = jnp.concatenate([w_ref[0], w_ref[1], w_ref[2], w_ref[3], wo_ref[0]], axis=1)
    gates = jax.nn.sigmoid(dot(transposed(wo_ref[0]), zn_ref[0]))
    for pos in range(count):
        lanes = slice(pos * LANES, (pos + 1) * LANES)
        gate = gates[:, lanes]
        d_update = cot_ref[pos].astype(F32) * gate
        cg_ref[0, :, lanes] = d_update * (1.0 - gate)
        du_ref[0, :, lanes] = d_update.astype(BF16)
    d_outn = dot(wo_ref[1], du_ref[0])
    for pos in range(count):
        scr[pl.ds(pos, chans, stride=count), :] = d_outn[:, pos * LANES:(pos + 1) * LANES]
    dout_ref[...] = scr[...].reshape(chans, count, LANES)


def chunk_order(chips):
    half = chips // 2
    far = [half + (j ^ (half // 2)) for j in range(half)]
    near = list(range(1, half))
    return [step for pair in zip(far, near) for step in pair] + far[len(near):] + [0]


def chunk_chip(me_ref, k, chips):
    return jnp.bitwise_xor(me_ref[0] // 2, chunk_order(chips)[k])


def collect_kernel(after_ref, *refs):
    *in_refs, out_ref = refs
    per = out_ref.shape[1]
    for k, ref in enumerate(in_refs):
        out_ref[k] = ref[per:2 * per]


def slice_rows(values, t, rows):
    chips, _, width = values.shape
    return values[:, t * rows:(t + 1) * rows].reshape(chips * rows, width).astype(BF16)


def mixed_kernel(rows, chips, me_ref, *refs):
    cols_refs, (own_ref, got_ref, out_ref, left_ref, right_ref, scr) = refs[:chips], refs[chips:]
    per, count, width = own_ref.shape[1:]
    templ, core = count // rows, me_ref[0] % 2
    for c in range(per):
        left_all = jnp.stack([ref[c].astype(F32) for ref in cols_refs])
        own, got = own_ref[:, c].astype(F32), got_ref[:, c].astype(F32)
        parts = []
        for t in range(templ):
            s = c * templ + t
            left = slice_rows(left_all, t, rows)
            left_ref[s] = left
            for k in range(chips):
                chip = chunk_chip(me_ref, k, chips)
                for values, half in ((own, core), (got, 1 - core)):
                    start = pl.multiple_of((chip * 2 + half) * rows, rows)
                    scr[s, pl.ds(start, rows), :] = values[k, t * rows:(t + 1) * rows]
            right = scr[s].astype(BF16)
            right_ref[s] = right
            parts.append(dot_nt(left, right).reshape(chips, rows, width))
        mixed = jnp.concatenate(parts, axis=1).astype(BF16)
        for k in range(chips):
            out_ref[chunk_chip(me_ref, k, chips), c] = mixed[k]


def triangle_back_kernel(rows, me_ref, dmix_ref, left_ref, right_ref, d_left_ref, keep_ref, send_ref, scr):
    chips, per, count, width = d_left_ref.shape
    templ, core = count // rows, me_ref[0] % 2
    for c in range(per):
        dmix_all = jnp.stack([dmix_ref[chunk_chip(me_ref, k, chips), c].astype(F32) for k in range(chips)])
        parts = []
        for t in range(templ):
            s = c * templ + t
            dmix = slice_rows(dmix_all, t, rows)
            parts.append(dot(dmix, right_ref[s]).reshape(chips, rows, width))
            scr[s] = dot_tn(dmix, left_ref[s])
        d_left_ref[:, c] = jnp.concatenate(parts, axis=1).astype(BF16)
    for k in range(chips):
        chip = chunk_chip(me_ref, k, chips)
        for ref, half in ((keep_ref, core), (send_ref, 1 - core)):
            here = pl.ds(pl.multiple_of((chip * 2 + half) * rows, rows), rows)
            for c in range(per):
                both = jnp.concatenate([scr[c * templ + t, here, :] for t in range(templ)], axis=0)
                ref[k, c] = both.astype(ref.dtype)


def join_kernel(d_left_ref, keep_ref, got_ref, *out_refs):
    chips, per, _, _ = d_left_ref.shape
    for k in range(chips):
        out_refs[k][0:per] = d_left_ref[k]
        out_refs[k][per:2 * per] = (keep_ref[k] + got_ref[k].astype(F32)).astype(BF16)


def split(x):
    high = x.astype(BF16).astype(F32)
    return high, x - high


def tree_sum(parts):
    while len(parts) > 1:
        parts = [a + b for a, b in zip(parts[::2], parts[1::2])] + parts[len(parts) // 2 * 2:]
    return parts[0]


def channel_sums(chans, values, scale):
    accs = [None] * 4
    for c in range(chans):
        v = values(c)
        accs[c % 4] = v if accs[c % 4] is None else [a + b for a, b in zip(accs[c % 4], v)]
    return [tree_sum(list(parts)) * scale for parts in zip(*accs)]


def middle_kernel(block, gains_ref, dout_ref, mixed_ref, dmix_ref, stats_ref):
    chans = dout_ref.shape[0]
    inv = 1.0 / chans

    def mixed(c):
        return mixed_ref[c].astype(F32)

    def scaled(c):
        return dout_ref[c] * gains_ref[1, c]

    mean, mean_h = channel_sums(chans, lambda c: (mixed(c), scaled(c)), inv)

    def moments(c):
        centred = mixed(c) - mean
        return centred * centred, scaled(c) * centred

    variance, mean_p = channel_sums(chans, moments, inv)
    rstd = lax.rsqrt(variance + EPS)
    mean_p = mean_p * rstd

    stats_ref[0] = mean
    stats_ref[1] = rstd
    for c in range(chans):
        xhat = (mixed(c) - mean) * rstd
        dmix_ref[c] = (rstd * (scaled(c) - mean_h - xhat * mean_p)).astype(BF16)


def update_kernel(block, gains_ref, mixed_ref, dout_ref, stats_ref, zn_ref, cg_ref, du_ref, wo_ref, dgate_ref, grads_ref, scr, norm_scr, outn_scr):
    chans, count, _ = mixed_ref.shape
    mean, rstd = stats_ref[0], stats_ref[1]
    for c in range(chans):
        xhat = (mixed_ref[c].astype(F32) - mean) * rstd
        scr[c * count:(c + 1) * count, :] = xhat * gains_ref[1, c]
        norm_scr[c:c + 1, :] = jnp.sum(dout_ref[c] * xhat, axis=0, keepdims=True)
    for pos in range(count):
        span = slice(pos * LANES, (pos + 1) * LANES)
        outn_scr[:, span] = scr[pl.ds(pos, chans, stride=count), :].astype(BF16)
    update = dot(transposed(wo_ref[1]), outn_scr[...])
    d_gate = (cg_ref[0] * update).astype(BF16)
    dgate_ref[0] = d_gate
    gate_grad = dot_nt(zn_ref[0], d_gate)
    out_grad = dot_nt(outn_scr[...], du_ref[0])

    @pl.when(block() == 0)
    def _():
        grads_ref[...] = jnp.zeros_like(grads_ref)

    grads_ref[0:chans, 0:chans] += gate_grad
    grads_ref[0:chans, chans:2 * chans] += out_grad
    grads_ref[chans:chans + 1, 0:chans] += as_row(jnp.sum(norm_scr[...], axis=1, keepdims=True))


def gating_back_kernel(blocks, chips, block, me_ref, fac_ref, zn_ref, grads_ref, *refs):
    *in_refs, d_ref, keep_ref, send_ref, left_scr, right_scr, pack_scr = refs
    chans = zn_ref.shape[1]
    count = left_scr.shape[0] // chans
    if chips:
        per = chans // chips
        for k in range(chips):
            here = pl.ds(chunk_chip(me_ref, k, chips) * (per * count), per * count)
            left_scr[here, :] = in_refs[k][0:per].astype(F32).reshape(per * count, LANES)
            right_scr[here, :] = in_refs[k][per:2 * per].astype(F32).reshape(per * count, LANES)
    else:
        left_scr[...] = in_refs[0][:, 0].astype(F32).reshape(chans * count, LANES)
        right_scr[...] = in_refs[0][:, 1].astype(F32).reshape(chans * count, LANES)
    for pos in range(count):
        span = slice(pos * LANES, (pos + 1) * LANES)
        where = pl.ds(pos, chans, stride=count)
        d_left, d_right = left_scr[where, :], right_scr[where, :]
        for p in range(4):
            d = d_left if p < 2 else d_right
            d_ref[0, p * chans:(p + 1) * chans, span] = (d * fac_ref[0, p * chans:(p + 1) * chans, span]).astype(BF16)
    grads = dot_nt(zn_ref[0], d_ref[0])

    @pl.when(block() == 0)
    def _():
        pack_scr[...] = jnp.zeros_like(pack_scr)

    pack_scr[0:chans, :] += grads[:, 0:2 * chans]
    pack_scr[chans:2 * chans, :] += grads[:, 2 * chans:4 * chans]

    @pl.when(block() == blocks - 1)
    def _():
        for ref, half in ((keep_ref, me_ref[0] % 2), (send_ref, 1 - me_ref[0] % 2)):
            ref[0:chans, :] = pack_scr[pl.ds(pl.multiple_of(half * chans, 8), chans), :]
            ref[chans:, :] = grads_ref[pl.ds(pl.multiple_of(half * (chans // 2), 8), chans // 2), :]


def input_grad_kernel(block, d_ref, dgate_ref, normed_ref, wcat_ref, dzn_ref, norm_ref):
    chans = normed_ref.shape[1]
    d_zn = dot(wcat_ref[:, 0:4 * chans], d_ref[0]) + dot(wcat_ref[:, 4 * chans:5 * chans], dgate_ref[0])
    dzn_ref[0] = d_zn

    @pl.when(block() == 0)
    def _():
        norm_ref[...] = jnp.zeros_like(norm_ref)

    norm_ref[0:1, 0:chans] += as_row(jnp.sum(d_zn * normed_ref[0], axis=1, keepdims=True))
    norm_ref[1:2, 0:chans] += as_row(jnp.sum(d_zn, axis=1, keepdims=True))


def pair_grad_kernel(block, after_ref, dzn_ref, normed_ref, rstd_ref, gains_ref, pair_ref):
    gain = column(gains_ref[0:1, :])
    for pos in range(pair_ref.shape[0]):
        span = slice(pos * LANES, (pos + 1) * LANES)
        h = dzn_ref[0, :, span] * gain
        normed = normed_ref[0, :, span]
        mean_h = jnp.mean(h, axis=0, keepdims=True)
        mean_p = jnp.mean(h * normed, axis=0, keepdims=True)
        pair_ref[pos] = (rstd_ref[0, :, span] * (h - mean_h - normed * mean_p)).astype(BF16)


def combine_kernel(keep_ref, got_ref, norm_ref, grads_ref, out_ref):
    chans = grads_ref.shape[0] - 8
    high, low = split(jnp.concatenate([norm_ref[0:2, :], grads_ref[chans:chans + 1, :]], axis=0))
    rest = jnp.zeros((2, norm_ref.shape[1]), F32)
    block = jnp.concatenate([keep_ref[...] + got_ref[...], high, low, rest], axis=0).astype(BF16)
    for d in range(out_ref.shape[0]):
        out_ref[d] = block


def total_kernel(pack_ref, mine_ref):
    mine_ref[...] = tree_sum([pack_ref[d].astype(F32) for d in range(pack_ref.shape[0])])


def unpack_kernel(scale, me_ref, mine_ref, got_ref, proj_ref, out_ref, norms_ref):
    chans = proj_ref.shape[1]
    rows = chans + chans // 2
    odd = me_ref[0] % 2 == 1
    mine, got = mine_ref[...] * scale, got_ref[...] * scale
    for half, total in enumerate((jnp.where(odd, got, mine), jnp.where(odd, mine, got))):
        for p in range(2):
            lanes = slice(p * chans, (p + 1) * chans)
            proj_ref[2 * half + p] = total[0:chans, lanes]
            out_ref[p, half * (chans // 2):(half + 1) * (chans // 2)] = total[chans:rows, lanes]
    norm = (mine + got)[rows:rows + 6, 0:chans]
    norms_ref[...] = norm[0:3] + norm[3:6]


def exchange(x, groups=None):
    return lax.all_to_all(x, "row", split_axis=0, concat_axis=0, axis_index_groups=groups, tiled=True)


def per_device(n, pair, cotangent, token_mask, coverage, w_proj, w_out, layer_norm_gains, ln_bias):
    templ, rows, chans, width = pair.shape
    count = templ * rows
    blocks = width // LANES
    chips = n // 2
    direct = blocks == 1 and n % 2 == 0 and chips & (chips - 1) == 0 and chans % chips == 0
    per = chans // chips if direct else 1
    lanes = count * LANES
    me = lax.axis_index("row").astype(jnp.int32).reshape(1)
    tokens_row = token_mask.reshape(1, width)

    params = pltpu.CompilerParams(vmem_limit_bytes=(16 if blocks == 1 else 40) * 1024 * 1024)
    smem = pl.BlockSpec(memory_space=pltpu.SMEM)
    whole = pl.BlockSpec(memory_space=pltpu.VMEM)

    def block_spec(shape, index):
        return whole if blocks == 1 else pl.BlockSpec(shape, index)

    def full(shape):
        return block_spec(shape, lambda b: (0,) * len(shape))

    def array(shape, dtype):
        return pltpu.VMEM(shape, dtype) if blocks == 1 else jax.ShapeDtypeStruct(shape, dtype)

    def from_hbm(x):
        return pltpu.with_memory_space_constraint(x, pltpu.HBM)

    def call(name, kernel, args, in_specs, out_specs, out_shape, scratch_shapes=()):
        block = (lambda: 0) if blocks == 1 else (lambda: pl.program_id(0))
        kernel = functools.partial(kernel, block)
        return pl.pallas_call(
            kernel,
            grid=() if blocks == 1 else (blocks,),
            in_specs=in_specs,
            out_specs=out_specs,
            out_shape=out_shape,
            scratch_shapes=scratch_shapes,
            compiler_params=params,
            name=name,
        )(*args)

    rows_spec = block_spec((count, chans, LANES), lambda b: (0, 0, b))
    tok_spec = block_spec((1, LANES), lambda b: (0, b))
    lr_spec = block_spec((chans, 2, count, LANES), lambda b: (0, 0, 0, b))
    cat_spec = block_spec((1, chans, lanes), lambda b: (b, 0, 0))
    fac_spec = block_spec((1, 4 * chans, lanes), lambda b: (b, 0, 0))
    one_spec = block_spec((1, 1, lanes), lambda b: (b, 0, 0))
    chan_spec = block_spec((chans, count, LANES), lambda b: (0, 0, b))
    w_spec, wo_spec, gains_spec = full(w_proj.shape), full(w_out.shape), full(layer_norm_gains.shape)
    scratch = pltpu.VMEM((chans * count, LANES), F32)
    pair_rows = from_hbm(pair.reshape(count, chans, width))
    cot_rows = from_hbm(cotangent.reshape(count, chans, width))
    w_proj_in, w_out_in, gains_in = from_hbm(w_proj), from_hbm(w_out), from_hbm(layer_norm_gains)
    tokens_in, cover_in = from_hbm(tokens_row), from_hbm(coverage.transpose(1, 2, 0))

    def cat(dtype):
        return array((blocks, chans, lanes), dtype)

    def chunks(depth):
        return [jax.ShapeDtypeStruct((depth, count, width), BF16)] * chips

    def send_chunks(parts):
        return [
            lax.ppermute(part, "row", [(d, d ^ (2 * step)) for d in range(n)]) if step else part
            for part, step in zip(parts, chunk_order(chips))
        ]

    *projected, zn, fac, normed, rstd = call(
        "project",
        functools.partial(project_kernel, rows, chips if direct else 0),
        (me, tokens_in, cover_in, pair_rows, tokens_in, w_proj_in, gains_in, from_hbm(ln_bias.reshape(1, chans))),
        [smem, full((1, width)), full(cover_in.shape), rows_spec, tok_spec, w_spec, gains_spec, full((1, chans))],
        ([whole] * chips if direct else [lr_spec]) + [cat_spec, fac_spec, cat_spec, one_spec],
        (chunks(2 * per) if direct else [jax.ShapeDtypeStruct((chans, 2, count, width), BF16)])
        + [cat(BF16), array((blocks, 4 * chans, lanes), F32), cat(F32), array((blocks, 1, lanes), F32)],
        [scratch, scratch],
    )
    if direct:
        cols = send_chunks(projected)

    cg, d_update, d_outn, wcat = call(
        "prepare",
        prepare_kernel,
        (cot_rows, zn, w_proj_in, w_out_in),
        [rows_spec, cat_spec, w_spec, wo_spec],
        [cat_spec, cat_spec, chan_spec, full((chans, 5 * chans))],
        [cat(F32), cat(BF16), array((chans, count, width), F32), array((chans, 5 * chans), BF16)],
        [scratch],
    )

    partner = [(d, d ^ 1) for d in range(n)]
    same_core = [list(range(core, n, 2)) for core in range(2)]
    if direct:
        slices = per * templ
        split_shape = (chips, per, count, width)
        square = pltpu.VMEM((slices, width, width), F32)
        own = pl.pallas_call(
            collect_kernel,
            in_specs=[pl.BlockSpec(memory_space=pl.ANY)] + [whole] * chips,
            out_shape=jax.ShapeDtypeStruct(split_shape, BF16),
            compiler_params=params,
            name="collect",
        )(wcat, *cols)
        got = lax.ppermute(own, "row", partner)
        mixed, left_cols, right_cols = pl.pallas_call(
            functools.partial(mixed_kernel, rows, chips),
            in_specs=[smem] + [whole] * (chips + 2),
            out_shape=[
                jax.ShapeDtypeStruct(split_shape, BF16),
                array((slices, chips * rows, width), BF16),
                array((slices, width, width), BF16),
            ],
            scratch_shapes=[square],
            compiler_params=params,
            name="mixed",
        )(me, *cols, own, got)
        mixed_rows = exchange(mixed, same_core).reshape(chans, count, width)
    else:
        slices = chans * templ // n
        cols = projected[0].reshape(chans, 2, templ, rows, width).transpose(0, 2, 1, 3, 4)
        cols = exchange(cols.reshape(n * slices, 2, rows, width)).reshape(n, slices, 2, rows, width)
        left_cols, right_cols = cols.transpose(2, 1, 0, 3, 4).reshape(2, slices, width, width)
        mixed = jnp.einsum("sik,sjk->sij", left_cols, right_cols, preferred_element_type=F32)
        mixed = mixed.astype(BF16).reshape(slices, n, rows, width).transpose(1, 0, 2, 3)
        mixed_rows = exchange(mixed.reshape(n * slices, rows, width)).reshape(chans, count, width)

    stats_spec = block_spec((2, count, LANES), lambda b: (0, 0, b))
    d_mixed, stats = call(
        "middle",
        middle_kernel,
        (layer_norm_gains, d_outn, mixed_rows),
        [smem, chan_spec, chan_spec],
        [chan_spec, stats_spec],
        [
            jax.ShapeDtypeStruct((chans, count, width), BF16),
            array((2, count, width), F32),
        ],
    )
    if direct:
        dmix_cols = exchange(d_mixed.reshape(split_shape), same_core)

    d_gate, out_grads = call(
        "update",
        update_kernel,
        (layer_norm_gains, mixed_rows, d_outn, stats, zn, cg, d_update, w_out),
        [smem, chan_spec, chan_spec, stats_spec, cat_spec, cat_spec, cat_spec, wo_spec],
        [cat_spec, full((chans + 8, 2 * chans))],
        [cat(BF16), array((chans + 8, 2 * chans), F32)],
        [scratch, pltpu.VMEM((chans, LANES), F32), pltpu.VMEM((chans, lanes), BF16)],
    )

    if direct:
        d_left, keep, send = pl.pallas_call(
            functools.partial(triangle_back_kernel, rows),
            in_specs=[smem] + [whole] * 3,
            out_shape=[array(split_shape, BF16), array(split_shape, F32), jax.ShapeDtypeStruct(split_shape, BF16)],
            scratch_shapes=[square],
            compiler_params=params,
            name="triangle_back",
        )(me, dmix_cols, left_cols, right_cols)
        got = lax.ppermute(send, "row", partner)
        d_lr = pl.pallas_call(
            join_kernel,
            out_shape=chunks(2 * per),
            compiler_params=params,
            name="join",
        )(d_left, keep, got)
        d_lr = send_chunks(d_lr)
    else:
        dmix_cols = exchange(d_mixed.reshape(n * slices, rows, width)).reshape(n, slices, rows, width)
        dmix_cols = dmix_cols.transpose(1, 0, 2, 3).reshape(slices, width, width)
        d_left = jnp.einsum("sij,sjk->sik", dmix_cols, right_cols, preferred_element_type=F32)
        d_right = jnp.einsum("sij,sik->sjk", dmix_cols, left_cols, preferred_element_type=F32)
        d_lr = jnp.stack([d_left.astype(BF16), d_right.astype(BF16)]).reshape(2, slices, n, rows, width)
        d_lr = exchange(d_lr.transpose(2, 1, 0, 3, 4).reshape(n * slices, 2, rows, width))
        d_lr = d_lr.reshape(chans, templ, 2, rows, width).transpose(0, 2, 1, 3, 4)
        d_lr = [d_lr.reshape(chans, 2, count, width)]

    half_rows = chans + chans // 2
    d_spec = block_spec((1, 4 * chans, lanes), lambda b: (b, 0, 0))
    d_pre, keep, send = call(
        "gating_back",
        functools.partial(gating_back_kernel, blocks, chips if direct else 0),
        (me, fac, zn, out_grads, *d_lr),
        [smem, fac_spec, cat_spec, full((chans + 8, 2 * chans))] + ([whole] * chips if direct else [lr_spec]),
        [d_spec, full((half_rows, 2 * chans)), full((half_rows, 2 * chans))],
        [
            array((blocks, 4 * chans, lanes), BF16),
            array((half_rows, 2 * chans), F32),
            jax.ShapeDtypeStruct((half_rows, 2 * chans), F32),
        ],
        [scratch, scratch, pltpu.VMEM((2 * chans, 2 * chans), F32)],
    )
    got = lax.ppermute(send, "row", partner)
    d_zn, norm_rows = call(
        "input_grad",
        input_grad_kernel,
        (d_pre, d_gate, normed, wcat),
        [d_spec, cat_spec, cat_spec, full((chans, 5 * chans))],
        [cat_spec, full((8, 2 * chans))],
        [cat(F32), array((8, 2 * chans), F32)],
    )
    sums = pl.pallas_call(
        combine_kernel,
        out_shape=jax.ShapeDtypeStruct((chips, half_rows + 8, 2 * chans), BF16),
        compiler_params=params,
        name="combine",
    )(keep, got, norm_rows, out_grads)
    sums = exchange(sums, same_core)
    mine = pl.pallas_call(
        total_kernel,
        out_shape=jax.ShapeDtypeStruct((half_rows + 8, 2 * chans), F32),
        compiler_params=params,
        name="total",
    )(sums)
    got = lax.ppermute(mine, "row", partner)
    pair_grad = call(
        "pair_grad",
        pair_grad_kernel,
        (mine, d_zn, normed, rstd, layer_norm_gains),
        [pl.BlockSpec(memory_space=pl.ANY), cat_spec, cat_spec, one_spec, gains_spec],
        rows_spec,
        jax.ShapeDtypeStruct((count, chans, width), BF16),
    )
    grad_proj, grad_out, norm_grads = pl.pallas_call(
        functools.partial(unpack_kernel, 1.0 / width),
        in_specs=[smem] + [whole] * 2,
        out_shape=[
            jax.ShapeDtypeStruct(w_proj.shape, F32),
            jax.ShapeDtypeStruct(w_out.shape, F32),
            jax.ShapeDtypeStruct((3, chans), F32),
        ],
        compiler_params=params,
        name="unpack",
    )(me, mine, got)
    return pair_grad.reshape(pair.shape), grad_proj, grad_out, norm_grads


def solution(mesh):
    return jax.shard_map(
        functools.partial(per_device, mesh.shape["row"]),
        mesh=mesh,
        in_specs=(
            P("groups", "row", None, None),
            P("groups", "row", None, None),
            P("groups"),
            P("groups", None, None),
            P(),
            P(),
            P(),
            P(),
        ),
        out_specs=(
            P("groups", "row", None, None),
            P("groups", None, None),
            P("groups", None, None),
            P("groups", None),
        ),
        check_vma=False,
    )
```
